256 devices in a mesh: dp: 16 (over y, z_hi), tensor: 16 (over z_lo, x, core).
Axes of the slice: x: 4, y: 4, z: 8 (z_hi: 4, z_lo: 2; z = z_hi * 2 + z_lo), core: 2. Of those that a mesh axis runs over, the one named last changes fastest.
Arguments:
- tokens_in: bfloat16 [2, 384, 5120], P(None, 'dp'), may hold values from -6 to 6
- attn_gain: float32 [5120], replicated, may hold values from 0.5 to 1.5
- post_gain: float32 [5120], replicated, may hold values from 0.5 to 1.5
- w_query: bfloat16 [5120, 4096], P(None, 'tensor'), may hold values from -0.078125 to 0.078125
- key_weight_base: bfloat16 [5120, 2048], P(None, 'tensor'), may hold values from -0.078125 to 0.078125
- value_weight_base: bfloat16 [5120, 2048], P(None, 'tensor'), may hold values from -0.078125 to 0.078125
- w_out: bfloat16 [4096, 5120], P('tensor'), may hold values from -0.09375 to 0.09375
- left_qkv: float32 [3, 5120, 64], P(None, 'dp'), may hold values from -0.078125 to 0.078125
- right_query: float32 [64, 4096], P('dp', 'tensor'), may hold values from -0.75 to 0.75
- right_key_value: float32 [2, 64, 2048], P(None, 'dp', 'tensor'), may hold values from -0.75 to 0.75
- left_out: float32 [4096, 64], P('tensor', 'dp'), may hold values from -0.09375 to 0.09375
- right_out: float32 [64, 5120], P('dp'), may hold values from -0.75 to 0.75
- kv_cache: bfloat16 [2, 384, 16, 320, 128], P(None, 'dp', 'tensor'), may hold values from -410 to 410
- lengths: int32 [384], P('dp'), may hold values from 1 to 320, as said below
- starts: int32 [384], P('dp'), may hold values from 0 to 319
Outputs:
- hidden_out: bfloat16 [2, 384, 5120], P(None, 'dp')
- mlp_input: bfloat16 [2, 384, 5120], P(None, 'dp')
- new_kv: bfloat16 [2, 2, 384, 2048], P(None, None, 'dp', 'tensor')
The draws below stay inside these ranges and needn't reach their ends.
Inputs may be any that keep to these rules, and one draw needn't show every extreme that they name: `lengths`: some rollout has exactly 320 cached tokens.
All inputs are finite; a program needn't handle non-finite values.
Results may differ from the reference program's by a relative error of at most 0.012.
The reference program's roundings to bfloat16 on the way count: a program that leaves them out, or rounds other values in their place, can miss the bound.
Values may be sent and summed in bfloat16 or wider, within the bound.
A program may use at most 128 MiB of HBM per device.

```python
import math
import jax
import jax.numpy as jnp
from jax import lax

MODEL_WIDTH = 5120
HQ = 32
KEY_VALUE_HEADS = 16
HEAD_WIDTH = 128
UPDATE_RANK = 64
CACHE_SLOTS = 320
WINDOW = 256
ROLLOUT_TOTAL = 384


def draw_lengths(key, part):
    key = jax.random.fold_in(key, 11)
    first_key, second_key = jax.random.split(key)
    drawn = jax.random.randint(first_key, (ROLLOUT_TOTAL,), 1, CACHE_SLOTS + 1, dtype=jnp.int32)
    longest = jax.random.randint(second_key, (), 0, ROLLOUT_TOTAL, dtype=jnp.int32)
    return drawn.at[longest].set(CACHE_SLOTS)


def draw_kv_cache(key, part):
    key = jax.random.fold_in(key, 23)
    base_key = jax.random.fold_in(key, 0)
    complete_shape = (2, ROLLOUT_TOTAL, KEY_VALUE_HEADS, CACHE_SLOTS, HEAD_WIDTH)
    values = jax.random.normal(base_key, complete_shape, jnp.float32)
    return values.astype(jnp.bfloat16)


def plant(array, rng, low, largest):
    index_at = [jax.random.randint(jax.random.fold_in(rng, axis), (), 0, length) for axis, length in enumerate(array.shape)]
    widest = array.shape.index(max(array.shape))
    beside = index_at[:widest] + [(index_at[widest] + 1) % array.shape[widest]] + index_at[widest + 1:]
    return array.at[tuple(index_at)].set(low).at[tuple(beside)].set(largest)


def shard_levels(key, shape, cuts, low, largest):
    gain = 1.0
    for dim, shards_of in cuts:
        heights = jax.random.uniform(jax.random.fold_in(jax.random.fold_in(key, 6), dim), (shards_of,), jnp.float32, low / len(cuts), largest / len(cuts))
        gain = gain * jnp.repeat(jnp.exp(heights), shape[dim] // shards_of).reshape((-1,) + (1,) * (len(shape) - 1 - dim))
    return gain


def normal_values(key, shape, width, bound, shards=(), kind=jnp.bfloat16):
    values = width * jax.random.normal(key, shape, jnp.float32)
    if shards:
        values = values * shard_levels(key, shape, shards, -0.22, 0.18)
    return jnp.clip(values, -bound, bound).astype(kind)


def setup_inputs(seed: int = 0) -> dict:
    key_of = jax.random.split(jax.random.key(seed), 16)
    return {
        "tokens_in": normal_values(key_of[0], (2, ROLLOUT_TOTAL, MODEL_WIDTH), 1.0, 6.0, ((1, 16),)),
        "attn_gain": jnp.clip(1.0 + 0.1 * jax.random.normal(key_of[1], (MODEL_WIDTH,), jnp.float32), 0.5, 1.5),
        "post_gain": jnp.clip(1.0 + 0.1 * jax.random.normal(key_of[2], (MODEL_WIDTH,), jnp.float32), 0.5, 1.5),
        "w_query": normal_values(key_of[3], (MODEL_WIDTH, HQ * HEAD_WIDTH), MODEL_WIDTH ** -0.5, 0.078125, ((1, 16),)),
        "key_weight_base": normal_values(key_of[4], (MODEL_WIDTH, KEY_VALUE_HEADS * HEAD_WIDTH), MODEL_WIDTH ** -0.5, 0.078125, ((1, 16),)),
        "value_weight_base": normal_values(key_of[5], (MODEL_WIDTH, KEY_VALUE_HEADS * HEAD_WIDTH), MODEL_WIDTH ** -0.5, 0.078125, ((1, 16),)),
        "w_out": normal_values(key_of[6], (HQ * HEAD_WIDTH, MODEL_WIDTH), (HQ * HEAD_WIDTH) ** -0.5, 0.09375, ((0, 16),)),
        "left_qkv": normal_values(key_of[7], (3, MODEL_WIDTH, UPDATE_RANK), MODEL_WIDTH ** -0.5, 0.078125, ((1, 16),), jnp.float32),
        "right_query": normal_values(key_of[8], (UPDATE_RANK, HQ * HEAD_WIDTH), UPDATE_RANK ** -0.5, 0.75, ((0, 16), (1, 16)), jnp.float32),
        "right_key_value": normal_values(key_of[9], (2, UPDATE_RANK, KEY_VALUE_HEADS * HEAD_WIDTH), UPDATE_RANK ** -0.5, 0.75, ((1, 16), (2, 16)), jnp.float32),
        "left_out": normal_values(key_of[10], (HQ * HEAD_WIDTH, UPDATE_RANK), (HQ * HEAD_WIDTH) ** -0.5, 0.09375, ((0, 16), (1, 16)), jnp.float32),
        "right_out": normal_values(key_of[11], (UPDATE_RANK, MODEL_WIDTH), UPDATE_RANK ** -0.5, 0.75, ((0, 16),), jnp.float32),
        "kv_cache": draw_kv_cache(jax.random.fold_in(key_of[15], 71), 0),
        "lengths": draw_lengths(jax.random.fold_in(key_of[15], 71), 0),
        "starts": plant(jax.random.randint(key_of[14], (ROLLOUT_TOTAL,), 0, CACHE_SLOTS), jax.random.fold_in(key_of[14], 1), 0, CACHE_SLOTS - 1).astype(jnp.int32),
    }


ROPE_BASE = 1000000.0

def apply_rotary(vectors, token_positions):
    half_size = vectors.shape[-1] // 2
    inverse_freq = ROPE_BASE ** (-(jnp.arange(half_size, dtype=jnp.float32) * 2.0 / vectors.shape[-1]))
    angles = token_positions.astype(jnp.float32)[:, None] * inverse_freq[None, :]
    cosine = jnp.cos(angles)[:, None, :]
    sine_part = jnp.sin(angles)[:, None, :]
    lower_half = vectors[..., :half_size]
    upper_half = vectors[..., half_size:]
    return jnp.concatenate([lower_half * cosine - upper_half * sine_part, upper_half * cosine + lower_half * sine_part], -1)

def normalize(values, gains):
    return values * lax.rsqrt(lax.optimization_barrier(jnp.mean(values * values, -1, keepdims=True)) + 1e-06) * gains

def merge_weight(base_weight, left_part, right_part):
    update = jnp.dot(left_part, right_part, precision=lax.Precision.HIGHEST)
    return (base_weight.astype(jnp.float32) + 0.5 * update).astype(jnp.bfloat16)

def attend(queries, cache_keys, cache_vals, fresh_keys, fresh_vals, lengths, starts, token_positions):
    batch_rows, head_count, head_size = queries.shape
    kv_count = cache_keys.shape[1]
    slot_count = cache_keys.shape[2]
    grouped = queries.astype(jnp.float32).reshape(batch_rows, kv_count, head_count // kv_count, head_size)
    scale_factor = 1.0 / math.sqrt(head_size)
    cached_scores = jnp.einsum('bkgd,bkcd->bkgc', grouped, cache_keys.astype(jnp.float32)) * scale_factor
    fresh_scores = jnp.einsum('bkgd,bked->bkge', grouped, fresh_keys.astype(jnp.float32)) * scale_factor
    slot_ids = jnp.arange(slot_count, dtype=jnp.int32)
    logical = (slot_ids[None, :] - starts[:, None]) % slot_count
    visible = (logical < lengths[:, None]) & (token_positions[:, None] - logical < WINDOW)
    cached_scores = jnp.where(visible[:, None, None, :], cached_scores, -1e+30)
    row_max = jnp.maximum(lax.optimization_barrier(jnp.max(cached_scores, -1, keepdims=True)), lax.optimization_barrier(jnp.max(fresh_scores, -1, keepdims=True)))
    cached_exp = jnp.exp(cached_scores - row_max)
    fresh_exp = jnp.exp(fresh_scores - row_max)
    denominator = lax.optimization_barrier(jnp.sum(cached_exp, -1, keepdims=True)) + lax.optimization_barrier(jnp.sum(fresh_exp, -1, keepdims=True))
    cached_prob = (cached_exp / denominator).astype(jnp.bfloat16)
    fresh_prob = (fresh_exp / denominator).astype(jnp.bfloat16)
    blended = jnp.einsum('bkgc,bkcd->bkgd', cached_prob.astype(jnp.float32), cache_vals.astype(jnp.float32))
    blended = blended + jnp.einsum('bkge,bked->bkgd', fresh_prob.astype(jnp.float32), fresh_vals.astype(jnp.float32))
    return blended.reshape(batch_rows, head_count * head_size).astype(jnp.bfloat16)

def reference(tokens_in, attn_gain, post_gain, w_query, key_weight_base, value_weight_base, w_out, left_qkv, right_query, right_key_value, left_out, right_out, kv_cache, lengths, starts):
    merged_query = merge_weight(w_query, left_qkv[0], right_query)
    combined_key_weight = merge_weight(key_weight_base, left_qkv[1], right_key_value[0])
    combined_value_weight = merge_weight(value_weight_base, left_qkv[2], right_key_value[1])
    merged_out = merge_weight(w_out, left_out, right_out)
    fresh_keys = []
    fresh_vals = []
    hidden_list = []
    normed_list = []
    key_value_list = []
    for token_step in range(2):
        inputs = tokens_in[token_step].astype(jnp.float32)
        normalized_input = normalize(inputs, attn_gain).astype(jnp.bfloat16)
        token_positions = lengths + token_step
        queries = apply_rotary(jnp.dot(normalized_input, merged_query, preferred_element_type=jnp.float32).reshape(ROLLOUT_TOTAL, HQ, HEAD_WIDTH), token_positions).astype(jnp.bfloat16)
        incoming_keys = apply_rotary(jnp.dot(normalized_input, combined_key_weight, preferred_element_type=jnp.float32).reshape(ROLLOUT_TOTAL, KEY_VALUE_HEADS, HEAD_WIDTH), token_positions).astype(jnp.bfloat16)
        incoming_values = jnp.dot(normalized_input, combined_value_weight, preferred_element_type=jnp.float32).reshape(ROLLOUT_TOTAL, KEY_VALUE_HEADS, HEAD_WIDTH).astype(jnp.bfloat16)
        fresh_keys.append(incoming_keys)
        fresh_vals.append(incoming_values)
        attended = attend(queries, kv_cache[0], kv_cache[1], jnp.stack(fresh_keys, 2), jnp.stack(fresh_vals, 2), lengths, starts, token_positions)
        projected = jnp.dot(attended, merged_out, preferred_element_type=jnp.float32)
        hidden = (inputs + projected).astype(jnp.bfloat16)
        hidden_list.append(hidden)
        normed_list.append(normalize(hidden.astype(jnp.float32), post_gain).astype(jnp.bfloat16))
        key_value_list.append(jnp.stack([incoming_keys.reshape(ROLLOUT_TOTAL, KEY_VALUE_HEADS * HEAD_WIDTH), incoming_values.reshape(ROLLOUT_TOTAL, KEY_VALUE_HEADS * HEAD_WIDTH)]))
    return (jnp.stack(hidden_list), jnp.stack(normed_list), jnp.stack(key_value_list))
```

```python
import math

import jax
import jax.numpy as jnp
from jax import lax
from jax.experimental import pallas as pl
from jax.experimental.pallas import tpu as pltpu
from jax.sharding import PartitionSpec as P

MESH = pl.DeviceIdType.MESH
BF16 = jnp.bfloat16
F32 = jnp.float32

WIDTH = 5120
HEAD = 128
SLOTS = 320
WINDOW = 256
RANK = 64
ROWS = 24
DP = 16
TP = 16
CHIPS = 8
BLOCK = WIDTH // CHIPS
LROWS = WIDTH // DP
LPAD = 384
NT = (((1,), (1,)), ((), ()))
TN = (((0,), (0,)), ((), ()))
NN = (((1,), (0,)), ((), ()))


def dot(a, b, dims=NN):
    return lax.dot_general(a, b, dims, preferred_element_type=F32)


def iota(shape, axis):
    return lax.broadcasted_iota(jnp.int32, shape, axis)


def one_hot(cond):
    return jnp.where(cond, 1.0, 0.0).astype(BF16)


def main_kernel(
    tok_in, gain_in, wq_in, wk_in, wv_in, wo_in, lqkv_in, rq_in, rkv_in, lo_in, ro_in, kv_in,
    len_in, start_in,
    hid_out, kv_out,
    tok, gain, w, wo, kvc, lens, starts,
    lbuf, rq, rkv, lob, rob,
    lsend, lgat, pack, pkgat, zgat, rmat,
    normed, proj, qs, kx, vx, score, prob, att, att2,
    ybuf, ysend, yrecv, yall, keep, bsend, brecv, csend, crecv, hid,
    loc, lsend_sem, lrecv_sem, psend_sem, precv_sem, zsend_sem, zrecv_sem,
    ysend_sem, yrecv_sem, y2send_sem, y2recv_sem, bsend_sem, brecv_sem, csend_sem, crecv_sem,
    gsend_sem, grecv_sem, fsend_sem, frecv_sem,
):
    dp = lax.axis_index("dp")
    tp = lax.axis_index("tensor")
    chip = tp // 2
    core = tp % 2
    sib = tp + 1 - 2 * core
    other = 1 - core

    def load(src, dst, k):
        c = pltpu.make_async_copy(src, dst, loc.at[k])
        c.start()
        return c

    active = jnp.logical_or(tp < 8, core == 0)
    slab = jnp.where(tp < 8, tp, tp // 2 + 4)
    shift = 64 * (dp % 2)
    lbuf[0:64, :] = jnp.zeros((64, RANK), F32)
    lbuf[LROWS:LPAD, :] = jnp.zeros((LPAD - LROWS, RANK), F32)
    ld_l = load(lqkv_in.at[slab // 4], lbuf.at[pl.ds(pl.multiple_of(shift, 64), LROWS)], 0)
    ld_rq = load(rq_in, rq, 1)
    ld_rkv = load(rkv_in, rkv, 2)
    ld_lo = load(lo_in, lob, 3)
    ld_ro = load(ro_in.at[:, pl.ds(pl.multiple_of(chip * BLOCK, 128), BLOCK)], rob, 4)
    ld_tok = load(tok_in, tok, 5)
    ld_gain = load(gain_in, gain, 6)
    ld_len = load(len_in, lens, 7)
    ld_st = load(start_in, starts, 8)
    ld_w = []
    step = WIDTH // 4
    for i in range(4):
        rs = pl.ds(i * step, step)
        ld_w.append([
            load(wq_in.at[rs], w.at[rs, 0:256], 9 + 3 * i),
            load(wk_in.at[rs], w.at[rs, 256:384], 10 + 3 * i),
            load(wv_in.at[rs], w.at[rs, 384:512], 11 + 3 * i),
        ])
    ld_k = load(kv_in.at[0, :, 0], kvc.at[0], 21)
    ld_v = load(kv_in.at[1, :, 0], kvc.at[1], 22)
    ld_wo = load(wo_in, wo, 23)

    barrier = pltpu.get_barrier_semaphore()

    def greet(d, _):
        pl.semaphore_signal(
            barrier, inc=1, device_id={"dp": (dp + d) % DP}, device_id_type=MESH)
        pl.semaphore_signal(
            barrier, inc=1, device_id={"tensor": (tp + d) % TP}, device_id_type=MESH)
        return 0

    lax.fori_loop(1, DP, greet, 0)

    ld_l.wait()
    pick = one_hot(iota((16, RANK), 1) == iota((16, RANK), 0) + 16 * (slab % 4))
    lsend[...] = dot(pick, lbuf[...].astype(BF16), NT).astype(BF16)
    lgat[dp] = lsend[...]
    ld_rq.wait()
    ld_rkv.wait()
    ld_lo.wait()
    ld_ro.wait()
    eye = one_hot(iota((8, 4), 0) == iota((8, 4), 1))
    lot = dot(eye, lob[...].astype(BF16), NT)[0:4]
    tiles = [rq[:, 0:128], rq[:, 128:256], rkv[0], rkv[1], lot[:, 0:128], lot[:, 128:256]]
    tiles += [rob[:, 128 * i : 128 * (i + 1)] for i in range(5)]
    tiles += [jnp.zeros((4, 128), F32)]
    pack[...] = jnp.concatenate(tiles, 0).astype(BF16)
    pkgat[dp] = pack[...]

    pl.semaphore_wait(barrier, 2 * (DP - 1))

    def lcopy(d):
        to = (dp + d) % DP
        return pltpu.make_async_remote_copy(
            lsend, lgat.at[dp], lsend_sem.at[d], lrecv_sem.at[dp],
            device_id={"dp": to}, device_id_type=MESH)

    def pcopy(d):
        to = (dp + d) % DP
        return pltpu.make_async_remote_copy(
            pack, pkgat.at[dp], psend_sem.at[d], precv_sem.at[dp],
            device_id={"dp": to}, device_id_type=MESH)

    def send_l(d, _):
        lcopy(d).start()
        return 0

    def send_p(d, _):
        pcopy(d).start()
        return 0

    @pl.when(active)
    def _():
        lax.fori_loop(1, DP, send_l, 0)

    lax.fori_loop(1, DP, send_p, 0)

    ld_tok.wait()
    ld_gain.wait()
    sq = jnp.zeros((2, ROWS, 1), F32)
    for i in range(8):
        v = tok[:, :, i * 640 : (i + 1) * 640].astype(F32)
        sq = sq + jnp.sum(v * v, -1, keepdims=True)
    rs = lax.rsqrt(sq * (1.0 / WIDTH) + 1e-06)
    for i in range(8):
        cols = slice(i * 640, (i + 1) * 640)
        v = tok[:, :, cols].astype(F32) * rs * gain[:, cols][None]
        normed[:, cols] = v.reshape(2 * ROWS, 640).astype(BF16)

    acc = None
    for i in range(2):
        for c in ld_w[i]:
            c.wait()
        part = dot(normed[:, i * step : (i + 1) * step], w[i * step : (i + 1) * step, :])
        acc = part if acc is None else acc + part
    proj[...] = acc

    def zcopy(d, to, src, who):
        return pltpu.make_async_remote_copy(
            zgat.at[src], zgat.at[src], zsend_sem.at[d], zrecv_sem.at[src],
            device_id={"tensor": to}, device_id_type=MESH)

    @pl.when(active)
    def _():
        def got(d, _):
            src = (dp + d) % DP
            pltpu.make_async_copy(lgat.at[src], lgat.at[src], lrecv_sem.at[src]).wait()
            return 0

        lax.fori_loop(1, DP, got, 0)
        z = jnp.zeros((16, 2 * ROWS), F32)
        for j in range(DP):
            base = 640 * (j // 2) + 256 * (j % 2)
            z = z + dot(lgat[j], normed[:, base : base + LPAD], NT)
        z = jnp.concatenate([z, jnp.zeros((16, 128 - 2 * ROWS), F32)], 1)
        zgat[slab] = z.astype(BF16)

        def send_z(d, _):
            zcopy(d, (tp + d) % TP, slab, tp).start()
            return 0

        lax.fori_loop(1, TP, send_z, 0)

    acc = proj[...]
    for i in range(2, 4):
        for c in ld_w[i]:
            c.wait()
        acc = acc + dot(normed[:, i * step : (i + 1) * step], w[i * step : (i + 1) * step, :])
    proj[...] = acc

    ld_len.wait()
    ld_st.wait()
    lenf = lens[...].astype(F32)
    stf = starts[...].astype(F32)

    def column(values, rows, owner):
        hit = owner(iota((rows, ROWS), 0)) == iota((rows, ROWS), 1)
        return jnp.sum(jnp.where(hit, values, 0.0), -1, keepdims=True)

    row = iota((2 * ROWS, 1), 0)
    pos = column(lenf, 2 * ROWS, lambda r: r % ROWS) + jnp.where(row >= ROWS, 1.0, 0.0)
    lane = iota((1, HEAD), 1)
    freq = jnp.exp((lane % 64).astype(F32) * (-2.0 * math.log(1000000.0) / HEAD))
    angle = pos * freq
    cos = jnp.cos(angle)
    sin = jnp.sin(angle) * jnp.where(lane < 64, -1.0, 1.0)

    def rope(v):
        return v * cos + pltpu.roll(v, 64, 1) * sin

    arow = iota((4 * ROWS, 1), 0)
    tokstep = jnp.where(arow % 4 >= 2, 1.0, 0.0)
    alen = column(lenf, 4 * ROWS, lambda r: r // 4)
    ast = column(stf, 4 * ROWS, lambda r: r // 4)
    slot = iota((4 * ROWS, SLOTS), 1).astype(F32) - ast
    slot = jnp.where(slot < 0, slot + float(SLOTS), slot)
    visible = jnp.logical_and(slot < alen, alen + tokstep - slot < float(WINDOW))

    def gotp(d, _):
        src = (dp + d) % DP
        pltpu.make_async_copy(pkgat.at[src], pkgat.at[src], precv_sem.at[src]).wait()
        return 0

    lax.fori_loop(1, DP, gotp, 0)
    o = iota((256, 256), 0)
    perm = one_hot(iota((256, 256), 1) == ((o % 64) // 4) * 16 + 4 * (o // 64) + o % 4)
    for g in range(3):
        grp = pkgat[:, 16 * g : 16 * (g + 1), :].reshape(256, 128)
        rmat[g] = dot(perm, grp).astype(BF16)

    def gotz(s, _):
        src = jnp.where(s < 8, s, 2 * s - 8)

        @pl.when(src != tp)
        def _():
            pltpu.make_async_copy(zgat.at[s], zgat.at[s], zrecv_sem.at[s]).wait()

        return 0

    lax.fori_loop(0, 12, gotz, 0)
    cols = []
    for t, p in enumerate((0, 0, 1, 2)):
        z = zgat[4 * p : 4 * (p + 1)].reshape(RANK, 128)
        delta = dot(z, rmat[0, 64 * t : 64 * (t + 1), :], TN)[: 2 * ROWS]
        cols.append(proj[:, 128 * t : 128 * (t + 1)] + 0.5 * delta)
    rounded = [rope(cols[0]), rope(cols[1]), rope(cols[2]), cols[3]]
    rounded = [v.astype(BF16).astype(F32) for v in rounded]
    for t in range(2):
        rows = slice(t * ROWS, (t + 1) * ROWS)
        kv_out[t, 0] = rounded[2][rows].astype(BF16)
        kv_out[t, 1] = rounded[3][rows].astype(BF16)
        for g in range(2):
            qs[pl.ds(2 * t + g, ROWS, stride=4), :] = rounded[g][rows]
        for r in range(4):
            kx[t, pl.ds(r, ROWS, stride=4), :] = rounded[2][rows]
            vx[t, pl.ds(r, ROWS, stride=4), :] = rounded[3][rows]

    scale = 1.0 / math.sqrt(HEAD)
    ld_k.wait()
    which = iota((16, 1), 0) // 4
    for i in range(6):
        q = qs[16 * i : 16 * (i + 1), :].astype(BF16)
        s = dot(q, kvc[0, 4 * i], NT)
        for b in range(1, 4):
            s = jnp.where(which == b, dot(q, kvc[0, 4 * i + b], NT), s)
        score[16 * i : 16 * (i + 1), :] = s
    sc = jnp.where(visible, score[...] * scale, -1e30)
    q = qs[...]
    f0 = jnp.sum(q * kx[0], -1, keepdims=True) * scale
    f1 = jnp.sum(q * kx[1], -1, keepdims=True) * scale
    f1 = jnp.where(tokstep > 0.5, f1, -1e30)
    top = jnp.maximum(jnp.max(sc, -1, keepdims=True), jnp.maximum(f0, f1))
    ex = jnp.exp(sc - top)
    e0 = jnp.exp(f0 - top)
    e1 = jnp.exp(f1 - top)
    den = jnp.sum(ex, -1, keepdims=True) + (e0 + e1)
    prob[...] = (ex / den).astype(BF16)
    p0 = (e0 / den).astype(BF16).astype(F32)
    p1 = (e1 / den).astype(BF16).astype(F32)
    att[...] = p0 * vx[0] + p1 * vx[1]
    ld_v.wait()
    for i in range(6):
        rows = slice(16 * i, 16 * (i + 1))
        p = prob[rows, :]
        s = dot(p, kvc[1, 4 * i])
        for b in range(1, 4):
            s = jnp.where(which == b, dot(p, kvc[1, 4 * i + b]), s)
        att[rows, :] = att[rows, :] + s
    for t in range(2):
        for g in range(2):
            att2[t, :, 128 * g : 128 * (g + 1)] = att[pl.ds(2 * t + g, ROWS, stride=4), :]
    attended = jnp.concatenate([att2[core], att2[other]], 0).astype(BF16)

    lot = jnp.concatenate([rmat[1, 0:64, :], rmat[1, 64:128, :]], 1)
    y = dot(attended, lot, NT)
    y = jnp.concatenate([y, jnp.zeros((2 * ROWS, 128 - RANK), F32)], 1)
    ybuf[...] = y[0:ROWS]
    ysend[0] = y[ROWS:].astype(BF16)
    ycopy = pltpu.make_async_remote_copy(
        ysend.at[0], yrecv, ysend_sem, yrecv_sem, device_id={"tensor": sib}, device_id_type=MESH)
    ycopy.start()

    def bcopy(n):
        return pltpu.make_async_remote_copy(
            bsend.at[n], brecv.at[n], bsend_sem.at[n], brecv_sem.at[n],
            device_id={"tensor": sib}, device_id_type=MESH)

    def ccopy(n):
        to = (chip + 1 + n) % CHIPS
        return pltpu.make_async_remote_copy(
            csend.at[n], crecv.at[chip], csend_sem.at[n], crecv_sem.at[chip],
            device_id={"tensor": 2 * to + core}, device_id_type=MESH)

    def y2copy(n):
        to = (chip + 1 + n) % CHIPS
        return pltpu.make_async_remote_copy(
            ysend.at[1], yall.at[chip], y2send_sem.at[n], y2recv_sem.at[chip],
            device_id={"tensor": 2 * to + core}, device_id_type=MESH)

    ld_wo.wait()
    for n in range(CHIPS):
        to = (chip + 1 + n) % CHIPS
        part = dot(attended, wo[:, pl.ds(pl.multiple_of(to * BLOCK, 128), BLOCK)])
        keep[n] = part[0:ROWS]
        bsend[n] = part[ROWS:].astype(BF16)
        bcopy(n).start()

    ycopy.wait_recv()
    ymine = ybuf[...] + yrecv[...].astype(F32)
    ysend[1] = ymine.astype(BF16)
    for n in range(CHIPS - 1):
        y2copy(n).start()
    for n in range(CHIPS - 1):
        bcopy(n).wait_recv()
        csend[n] = (keep[n] + brecv[n].astype(F32)).astype(BF16)
        ccopy(n).start()
    bcopy(CHIPS - 1).wait_recv()
    total = keep[CHIPS - 1] + brecv[CHIPS - 1].astype(F32)
    here = pl.ds(pl.multiple_of(chip * BLOCK, 128), BLOCK)
    total = total + tok[core, :, here].astype(F32)
    for n in range(CHIPS - 1):
        src = (chip + 1 + n) % CHIPS
        pltpu.make_async_copy(yall.at[src], yall.at[src], y2recv_sem.at[src]).wait()
        ymine = ymine + yall[src].astype(F32)
    ro = jnp.concatenate(
        [rmat[1, 128:192, :], rmat[1, 192:256, :], rmat[2, 0:64, :], rmat[2, 64:128, :],
         rmat[2, 128:192, :]], 1)
    total = total + 0.5 * dot(ymine[:, 0:RANK].astype(BF16), ro)
    for n in range(CHIPS - 1):
        src = (chip + 1 + n) % CHIPS
        pltpu.make_async_copy(crecv.at[src], crecv.at[src], crecv_sem.at[src]).wait()
        total = total + crecv[src].astype(F32)
    hid[core, :, here] = total.astype(BF16)

    def block(k, c):
        return hid.at[k, :, pl.ds(pl.multiple_of(c * BLOCK, 128), BLOCK)]

    def gcopy(n):
        to = (chip + 1 + n) % CHIPS
        return pltpu.make_async_remote_copy(
            block(core, chip), block(core, chip), gsend_sem.at[n], grecv_sem.at[chip],
            device_id={"tensor": 2 * to + core}, device_id_type=MESH)

    def fcopy(c):
        return pltpu.make_async_remote_copy(
            block(core, c), block(core, c), fsend_sem.at[c], frecv_sem.at[c],
            device_id={"tensor": sib}, device_id_type=MESH)

    for n in range(CHIPS - 1):
        gcopy(n).start()
    fcopy(chip).start()
    for n in range(CHIPS - 1):
        src = (chip + 1 + n) % CHIPS
        pltpu.make_async_copy(block(core, src), block(core, src), grecv_sem.at[src]).wait()
        fcopy(src).start()
    for n in range(CHIPS):
        c = (chip + n) % CHIPS
        pltpu.make_async_copy(block(other, c), block(other, c), frecv_sem.at[c]).wait()
    hid_out[...] = hid[...]

    @pl.when(active)
    def _():
        def done_l(d, _):
            lcopy(d).wait_send()
            return 0

        lax.fori_loop(1, DP, done_l, 0)

        def done_z(d, _):
            zcopy(d, (tp + d) % TP, slab, tp).wait_send()
            return 0

        lax.fori_loop(1, TP, done_z, 0)

    def done_p(d, _):
        pcopy(d).wait_send()
        return 0

    lax.fori_loop(1, DP, done_p, 0)
    ycopy.wait_send()
    for n in range(CHIPS):
        bcopy(n).wait_send()
        fcopy(n).wait_send()
    for n in range(CHIPS - 1):
        y2copy(n).wait_send()
        ccopy(n).wait_send()
        gcopy(n).wait_send()


def close_kernel(hid_ref, gain, kv_ref, hid_out, mlp_out, kv_out):
    kv_out[...] = kv_ref[...]
    sq = jnp.zeros((2, ROWS, 1), F32)
    for i in range(8):
        cols = slice(i * 640, (i + 1) * 640)
        v = hid_ref[:, :, cols]
        hid_out[:, :, cols] = v
        v = v.astype(F32)
        sq = sq + jnp.sum(v * v, -1, keepdims=True)
    rs = lax.rsqrt(sq * (1.0 / WIDTH) + 1e-06)
    for i in range(8):
        cols = slice(i * 640, (i + 1) * 640)
        v = hid_ref[:, :, cols].astype(F32) * rs * gain[:, cols][None]
        mlp_out[:, :, cols] = v.astype(BF16)


def shards(
    tokens_in, attn_gain, post_gain, w_query, key_weight_base, value_weight_base, w_out, left_qkv,
    right_query, right_key_value, left_out, right_out, kv_cache, lengths, starts,
):
    any_spec = pl.BlockSpec(memory_space=pl.ANY)
    vmem = pl.BlockSpec(memory_space=pltpu.VMEM)
    dma = pltpu.SemaphoreType.DMA
    scratch = [
        pltpu.VMEM((2, ROWS, WIDTH), BF16),
        pltpu.VMEM((1, WIDTH), F32),
        pltpu.VMEM((WIDTH, 512), BF16),
        pltpu.VMEM((256, WIDTH), BF16),
        pltpu.VMEM((2, ROWS, SLOTS, HEAD), BF16),
        pltpu.VMEM((1, ROWS), jnp.int32),
        pltpu.VMEM((1, ROWS), jnp.int32),
        pltpu.VMEM((LPAD, RANK), F32),
        pltpu.VMEM((4, 256), F32),
        pltpu.VMEM((2, 4, 128), F32),
        pltpu.VMEM((256, 4), F32),
        pltpu.VMEM((4, BLOCK), F32),
        pltpu.VMEM((16, LPAD), BF16),
        pltpu.VMEM((DP, 16, LPAD), BF16),
        pltpu.VMEM((48, 128), BF16),
        pltpu.VMEM((DP, 48, 128), BF16),
        pltpu.VMEM((12, 16, 128), BF16),
        pltpu.VMEM((3, 256, 128), BF16),
        pltpu.VMEM((2 * ROWS, WIDTH), BF16),
        pltpu.VMEM((2 * ROWS, 512), F32),
        pltpu.VMEM((4 * ROWS, HEAD), F32),
        pltpu.VMEM((2, 4 * ROWS, HEAD), F32),
        pltpu.VMEM((2, 4 * ROWS, HEAD), F32),
        pltpu.VMEM((4 * ROWS, SLOTS), F32),
        pltpu.VMEM((4 * ROWS, SLOTS), BF16),
        pltpu.VMEM((4 * ROWS, HEAD), F32),
        pltpu.VMEM((2, ROWS, 256), F32),
        pltpu.VMEM((ROWS, 128), F32),
        pltpu.VMEM((2, ROWS, 128), BF16),
        pltpu.VMEM((ROWS, 128), BF16),
        pltpu.VMEM((CHIPS, ROWS, 128), BF16),
        pltpu.VMEM((CHIPS, ROWS, BLOCK), F32),
        pltpu.VMEM((CHIPS, ROWS, BLOCK), BF16),
        pltpu.VMEM((CHIPS, ROWS, BLOCK), BF16),
        pltpu.VMEM((CHIPS, ROWS, BLOCK), BF16),
        pltpu.VMEM((CHIPS, ROWS, BLOCK), BF16),
        pltpu.VMEM((2, ROWS, WIDTH), BF16),
        dma((24,)),
        dma((DP,)), dma((DP,)), dma((DP,)), dma((DP,)), dma((TP,)), dma((12,)),
        dma, dma, dma((CHIPS,)), dma((CHIPS,)),
        dma((CHIPS,)), dma((CHIPS,)), dma((CHIPS,)), dma((CHIPS,)),
        dma((CHIPS,)), dma((CHIPS,)), dma((CHIPS,)), dma((CHIPS,)),
    ]
    hid, new_kv = pl.pallas_call(
        main_kernel,
        out_shape=(
            jax.ShapeDtypeStruct((2, ROWS, WIDTH), BF16),
            jax.ShapeDtypeStruct((2, 2, ROWS, HEAD), BF16),
        ),
        in_specs=[any_spec] * 14,
        out_specs=(vmem, vmem),
        scratch_shapes=scratch,
        compiler_params=pltpu.CompilerParams(
            collective_id=0, has_side_effects=True, vmem_limit_bytes=40 * 1024 * 1024),
    )(
        tokens_in, attn_gain.reshape(1, WIDTH), w_query, key_weight_base, value_weight_base, w_out,
        left_qkv, right_query, right_key_value, left_out, right_out, kv_cache,
        lengths.reshape(1, ROWS), starts.reshape(1, ROWS),
    )
    return pl.pallas_call(
        close_kernel,
        out_shape=(
            jax.ShapeDtypeStruct((2, ROWS, WIDTH), BF16),
            jax.ShapeDtypeStruct((2, ROWS, WIDTH), BF16),
            jax.ShapeDtypeStruct((2, 2, ROWS, HEAD), BF16),
        ),
        in_specs=[vmem] * 3,
        out_specs=(vmem, vmem, vmem),
    )(hid, post_gain.reshape(1, WIDTH), new_kv)


def solution(mesh):
    in_specs = (
        P(None, "dp", None),
        P(),
        P(),
        P(None, "tensor"),
        P(None, "tensor"),
        P(None, "tensor"),
        P("tensor", None),
        P(None, "dp", None),
        P("dp", "tensor"),
        P(None, "dp", "tensor"),
        P("tensor", "dp"),
        P("dp", None),
        P(None, "dp", "tensor", None, None),
        P("dp"),
        P("dp"),
    )
    out_specs = (P(None, "dp", None), P(None, "dp", None), P(None, None, "dp", "tensor"))
    return jax.shard_map(shards, mesh=mesh, in_specs=in_specs, out_specs=out_specs, check_vma=False)
```

```python
import math

import jax
import jax.numpy as jnp
from jax import lax
from jax.experimental import pallas as pl
from jax.experimental.pallas import tpu as pltpu
from jax.sharding import PartitionSpec as P

MESH = pl.DeviceIdType.MESH
BF16 = jnp.bfloat16
F32 = jnp.float32

WIDTH = 5120
HEAD = 128
SLOTS = 320
WINDOW = 256
RANK = 64
ROWS = 24
DP = 16
TP = 16
CHIPS = 8
XS = 4
HALF = WIDTH // 2
BLOCK = HALF // XS
LROWS = WIDTH // DP
LPAD = 384
NT = (((1,), (1,)), ((), ()))
TN = (((0,), (0,)), ((), ()))
NN = (((1,), (0,)), ((), ()))


def dot(a, b, dims=NN):
    return lax.dot_general(a, b, dims, preferred_element_type=F32)


def iota(shape, axis):
    return lax.broadcasted_iota(jnp.int32, shape, axis)


def one_hot(cond):
    return jnp.where(cond, 1.0, 0.0).astype(BF16)


def main_kernel(
    tok_in, gain_in, pgain_in, wq_in, wk_in, wv_in, wo_in, lqkv_in, rq_in, rkv_in, lo_in, ro_in,
    kv_in, len_in, start_in,
    hid_out, mlp_out, kv_out,
    tok, gain, pgain, w, wo, kvc, lens, starts,
    lbuf, rq, rkv, lob, rob,
    lsend, lgat, packa, packb, pagat, pbgat, zgat, rmat, losib,
    normed, proj, qs, kx, vx, score, prob, att, attboth, ysend, yall, csend, crecv, hid,
    loc, lsend_sem, lrecv_sem, asend_sem, arecv_sem, psend_sem, precv_sem, zsend_sem, zrecv_sem,
    sib_send, sib_recv, ysend_sem, yrecv_sem, csend_sem, crecv_sem,
    gsend_sem, grecv_sem, fsend_sem, frecv_sem,
):
    dp = lax.axis_index("dp")
    tp = lax.axis_index("tensor")
    chip = tp // 2
    core = tp % 2
    zlo = chip // XS
    xpos = chip % XS
    sib = tp + 1 - 2 * core
    other = 1 - core
    pend = {}

    def finish():
        for wait in pend.values():
            wait()

    def load(name, src, dst):
        c = pltpu.make_async_copy(src, dst, loc.at[len(pend)])
        c.start()
        pend[name] = c.wait

    def ready(*names):
        for name in names:
            pend.pop(name)()

    active = jnp.logical_or(tp < 8, core == 0)
    slab = jnp.where(tp < 8, tp, tp // 2 + 4)
    mine = core * HALF + xpos * BLOCK
    load("l", lqkv_in.at[slab // 4, pl.ds(pl.multiple_of(16 * (slab % 4), 16), 16)], lbuf)
    load("rq", rq_in, rq)
    load("rkv", rkv_in, rkv)
    load("lo", lo_in, lob)
    load("ro", ro_in.at[:, pl.ds(pl.multiple_of(mine, 128), BLOCK)], rob)
    load("tok", tok_in, tok)
    load("gain", gain_in, gain)
    load("len", len_in, lens)
    load("start", start_in, starts)
    step = WIDTH // 4
    for i in range(4):
        rs = pl.ds(i * step, step)
        load(("wq", i), wq_in.at[rs], w.at[rs, 0:256])
        load(("wk", i), wk_in.at[rs], w.at[rs, 256:384])
        load(("wv", i), wv_in.at[rs], w.at[rs, 384:512])
    load("k", kv_in.at[0, :, 0], kvc.at[0])
    load("v", kv_in.at[1, :, 0], kvc.at[1])
    load("wo", wo_in.at[:, pl.ds(pl.multiple_of(core * HALF, 128), HALF)], wo.at[0:256])
    load("pgain", pgain_in, pgain)

    barrier = pltpu.get_barrier_semaphore()

    def greet(d, _):
        pl.semaphore_signal(
            barrier, inc=1, device_id={"dp": (dp + d) % DP}, device_id_type=MESH)
        pl.semaphore_signal(
            barrier, inc=1, device_id={"tensor": (tp + d) % TP}, device_id_type=MESH)
        return 0

    lax.fori_loop(1, DP, greet, 0)

    ready("l")
    rank_rows = jnp.concatenate([lbuf[...], jnp.zeros((16, LPAD - LROWS), F32)], 1)
    rank_rows = jnp.where(dp % 2 == 1, pltpu.roll(rank_rows, LPAD - LROWS, 1), rank_rows)
    lsend[...] = rank_rows.astype(BF16)
    lgat[dp] = lsend[...]

    pl.semaphore_wait(barrier, 2 * (DP - 1))

    def gather(src, dst, send, recv, name):
        def copy(d):
            to = (dp + d) % DP
            return pltpu.make_async_remote_copy(
                src, dst.at[dp], send.at[d], recv.at[dp],
                device_id={"dp": to}, device_id_type=MESH)

        def go(d, _):
            copy(d).start()
            return 0

        def sent(d, _):
            copy(d).wait_send()
            return 0

        def got(d, _):
            who = (dp + d) % DP
            pltpu.make_async_copy(dst.at[who], dst.at[who], recv.at[who]).wait()
            return 0

        lax.fori_loop(1, DP, go, 0)
        pend[name, "sent"] = lambda: lax.fori_loop(1, DP, sent, 0)
        pend[name] = lambda: lax.fori_loop(1, DP, got, 0)

    def when_active(f):
        @pl.when(active)
        def _():
            f()

    @pl.when(active)
    def _():
        gather(lsend, lgat, lsend_sem, lrecv_sem, "L")

    lsent, lgot = pend.pop(("L", "sent")), pend.pop("L")
    pend["L", "sent"] = lambda: when_active(lsent)
    pend["L"] = lambda: when_active(lgot)

    ready("rq", "rkv")
    tiles = [rq[:, 0:128], rq[:, 128:256], rkv[0], rkv[1]]
    packa[...] = jnp.concatenate(tiles, 0).astype(BF16)
    pagat[dp] = packa[...]
    gather(packa, pagat, asend_sem, arecv_sem, "A")
    ready("lo", "ro")
    tiles = [lob[:, 0:128], lob[:, 128:256]]
    tiles += [rob[:, 128 * i : 128 * (i + 1)] for i in range(5)]
    tiles += [jnp.zeros((4, 128), F32)]
    packb[...] = jnp.concatenate(tiles, 0).astype(BF16)
    pbgat[dp] = packb[...]
    gather(packb, pbgat, psend_sem, precv_sem, "B")

    def to_sib(src, dst, k, name):
        c = pltpu.make_async_remote_copy(
            src, dst, sib_send.at[k], sib_recv.at[k],
            device_id={"tensor": sib}, device_id_type=MESH)
        c.start()
        pend[name, "sent"] = c.wait_send
        pend[name] = c.wait_recv

    to_sib(wo_in.at[:, pl.ds(pl.multiple_of(other * HALF, 128), HALF)], wo.at[256:512], 0, "wosib")


    ready("tok", "gain")
    sq = jnp.zeros((2, ROWS, 1), F32)
    for i in range(8):
        v = tok[:, :, i * 640 : (i + 1) * 640].astype(F32)
        sq = sq + jnp.sum(v * v, -1, keepdims=True)
    rs = lax.rsqrt(sq * (1.0 / WIDTH) + 1e-06)
    for i in range(8):
        cols = slice(i * 640, (i + 1) * 640)
        v = tok[:, :, cols].astype(F32) * rs * gain[:, cols][None]
        normed[:, cols] = v.reshape(2 * ROWS, 640).astype(BF16)

    acc = None
    for i in range(2):
        ready(("wq", i), ("wk", i), ("wv", i))
        part = dot(normed[:, i * step : (i + 1) * step], w[i * step : (i + 1) * step, :])
        acc = part if acc is None else acc + part
    proj[...] = acc

    ready("L")

    def zcopy(d):
        return pltpu.make_async_remote_copy(
            zgat.at[slab], zgat.at[slab], zsend_sem.at[d], zrecv_sem.at[slab],
            device_id={"tensor": (tp + d) % TP}, device_id_type=MESH)

    @pl.when(active)
    def _():
        parts = []
        for j in range(0, DP, 2):
            parts += [lgat[j, :, 0:256], lgat[j, :, 256:384] + lgat[j + 1, :, 0:128]]
            parts += [lgat[j + 1, :, 128:384]]
        z = dot(jnp.concatenate(parts, 1), normed[...], NT)
        z = jnp.concatenate([z, jnp.zeros((16, 128 - 2 * ROWS), F32)], 1)
        zgat[slab] = z.astype(BF16)

        def send_z(d, _):
            zcopy(d).start()
            return 0

        lax.fori_loop(1, TP, send_z, 0)

    def sent_z():
        def sent(d, _):
            zcopy(d).wait_send()
            return 0

        when_active(lambda: lax.fori_loop(1, TP, sent, 0))

    def got_z():
        def got(s, _):
            src = jnp.where(s < 8, s, 2 * s - 8)

            @pl.when(src != tp)
            def _():
                pltpu.make_async_copy(zgat.at[s], zgat.at[s], zrecv_sem.at[s]).wait()

            return 0

        lax.fori_loop(0, 12, got, 0)

    pend["Z", "sent"] = sent_z
    pend["Z"] = got_z
    acc = proj[...]
    for i in range(2, 4):
        ready(("wq", i), ("wk", i), ("wv", i))
        acc = acc + dot(normed[:, i * step : (i + 1) * step], w[i * step : (i + 1) * step, :])
    proj[...] = acc

    ready("len", "start")
    lenf = lens[...].astype(F32)
    stf = starts[...].astype(F32)

    def column(values, rows, owner):
        hit = owner(iota((rows, ROWS), 0)) == iota((rows, ROWS), 1)
        return jnp.sum(jnp.where(hit, values, 0.0), -1, keepdims=True)

    row = iota((2 * ROWS, 1), 0)
    pos = column(lenf, 2 * ROWS, lambda r: r % ROWS) + jnp.where(row >= ROWS, 1.0, 0.0)
    lane = iota((1, HEAD), 1)
    freq = jnp.exp((lane % 64).astype(F32) * (-2.0 * math.log(1000000.0) / HEAD))
    angle = pos * freq
    cos = jnp.cos(angle)
    sin = jnp.sin(angle) * jnp.where(lane < 64, -1.0, 1.0)

    def rope(v):
        return v * cos + pltpu.roll(v, 64, 1) * sin

    arow = iota((4 * ROWS, 1), 0)
    tokstep = jnp.where(arow % 4 >= 2, 1.0, 0.0)
    alen = column(lenf, 4 * ROWS, lambda r: r // 4)
    ast = column(stf, 4 * ROWS, lambda r: r // 4)
    slot = iota((4 * ROWS, SLOTS), 1).astype(F32) - ast
    slot = jnp.where(slot < 0, slot + float(SLOTS), slot)
    visible = jnp.logical_and(slot < alen, alen + tokstep - slot < float(WINDOW))

    ready("A")
    o = iota((256, 256), 0)
    perm = one_hot(iota((256, 256), 1) == ((o % 64) // 4) * 16 + 4 * (o // 64) + o % 4)
    rmat[0] = dot(perm, pagat[...].reshape(256, 128)).astype(BF16)

    ready("Z")
    cols = []
    for t, p in enumerate((0, 0, 1, 2)):
        z = zgat[4 * p : 4 * (p + 1)].reshape(RANK, 128)
        delta = dot(z, rmat[0, 64 * t : 64 * (t + 1), :], TN)[: 2 * ROWS]
        cols.append(proj[:, 128 * t : 128 * (t + 1)] + 0.5 * delta)
    rounded = [rope(cols[0]), rope(cols[1]), rope(cols[2]), cols[3]]
    rounded = [v.astype(BF16).astype(F32) for v in rounded]
    for t in range(2):
        rows = slice(t * ROWS, (t + 1) * ROWS)
        kv_out[t, 0] = rounded[2][rows].astype(BF16)
        kv_out[t, 1] = rounded[3][rows].astype(BF16)
        for g in range(2):
            qs[pl.ds(2 * t + g, ROWS, stride=4), :] = rounded[g][rows]
        for r in range(4):
            kx[t, pl.ds(r, ROWS, stride=4), :] = rounded[2][rows]
            vx[t, pl.ds(r, ROWS, stride=4), :] = rounded[3][rows]

    scale = 1.0 / math.sqrt(HEAD)
    ready("k")
    which = iota((16, 1), 0) // 4
    for i in range(6):
        q = qs[16 * i : 16 * (i + 1), :].astype(BF16)
        s = dot(q, kvc[0, 4 * i], NT)
        for b in range(1, 4):
            s = jnp.where(which == b, dot(q, kvc[0, 4 * i + b], NT), s)
        score[16 * i : 16 * (i + 1), :] = s
    sc = jnp.where(visible, score[...] * scale, -1e30)
    q = qs[...]
    f0 = jnp.sum(q * kx[0], -1, keepdims=True) * scale
    f1 = jnp.sum(q * kx[1], -1, keepdims=True) * scale
    f1 = jnp.where(tokstep > 0.5, f1, -1e30)
    top = jnp.maximum(jnp.max(sc, -1, keepdims=True), jnp.maximum(f0, f1))
    ex = jnp.exp(sc - top)
    e0 = jnp.exp(f0 - top)
    e1 = jnp.exp(f1 - top)
    den = jnp.sum(ex, -1, keepdims=True) + (e0 + e1)
    prob[...] = (ex / den).astype(BF16)
    p0 = (e0 / den).astype(BF16).astype(F32)
    p1 = (e1 / den).astype(BF16).astype(F32)
    att[...] = p0 * vx[0] + p1 * vx[1]
    ready("v")
    for i in range(6):
        rows = slice(16 * i, 16 * (i + 1))
        p = prob[rows, :]
        s = dot(p, kvc[1, 4 * i])
        for b in range(1, 4):
            s = jnp.where(which == b, dot(p, kvc[1, 4 * i + b]), s)
        att[rows, :] = att[rows, :] + s
    heads = []
    for g in range(2):
        heads.append(jnp.concatenate([att[pl.ds(2 * t + g, ROWS, stride=4), :] for t in range(2)], 0))
    attboth[0] = jnp.concatenate(heads, 1).astype(BF16)

    to_sib(attboth.at[0], attboth.at[1], 1, "att")
    ready("B")
    grp = pbgat[:, 0:16, :].reshape(256, 128)
    rmat[1] = dot(perm, grp).astype(BF16)
    losib[0] = rmat[1, 0:128, :]
    to_sib(losib.at[0], losib.at[1], 2, "losib")
    grp = pbgat[:, 16:32, :].reshape(256, 128)
    rmat[2] = dot(perm, grp).astype(BF16)

    def ccopy(c):
        return pltpu.make_async_remote_copy(
            csend.at[c], crecv.at[chip], csend_sem.at[c], crecv_sem.at[chip],
            device_id={"tensor": 2 * c + core}, device_id_type=MESH)

    def ycopy(c):
        return pltpu.make_async_remote_copy(
            ysend.at[c // XS], yall.at[chip], ysend_sem.at[c], yrecv_sem.at[chip],
            device_id={"tensor": 2 * c + core}, device_id_type=MESH)

    ready("wo", "wosib", "att")
    both = jnp.concatenate([attboth[0], attboth[1]], 1)
    total = None
    for n in (2, 1, 3, 0):
        x = (xpos + n) % XS
        part = dot(both, wo[:, pl.ds(pl.multiple_of(x * BLOCK, 128), BLOCK)])
        for t in range(2):
            csend[t * XS + x] = part[t * ROWS : (t + 1) * ROWS].astype(BF16)
            if n != 0:
                ccopy(t * XS + x).start()
        if n == 0:
            ccopy((1 - zlo) * XS + x).start()
            total = jnp.where(zlo == 0, part[0:ROWS], part[ROWS:])

    def peers(f):
        def body(n, _):
            f((chip + n) % CHIPS)
            return 0

        lax.fori_loop(1, CHIPS, body, 0)

    pend["C", "sent"] = lambda: peers(lambda c: ccopy(c).wait_send())

    ready("losib")
    lot = jnp.concatenate([losib[0, 0:64], losib[0, 64:128], losib[1, 0:64], losib[1, 64:128]], 1)
    y = dot(both, lot, NT)
    y = jnp.concatenate([y, jnp.zeros((2 * ROWS, 128 - RANK), F32)], 1)
    ysend[0] = y[0:ROWS].astype(BF16)
    ysend[1] = y[ROWS:].astype(BF16)
    peers(lambda c: ycopy(c).start())
    pend["Y", "sent"] = lambda: peers(lambda c: ycopy(c).wait_send())
    total = total + tok[zlo, :, pl.ds(pl.multiple_of(mine, 128), BLOCK)].astype(F32)
    ysum = jnp.where(zlo == 0, y[0:ROWS], y[ROWS:])
    for n in range(1, CHIPS):
        src = (chip + n) % CHIPS
        pltpu.make_async_copy(yall.at[src], yall.at[src], yrecv_sem.at[src]).wait()
        ysum = ysum + yall[src].astype(F32)
    ro = jnp.concatenate(
        [rmat[1, 128:192, :], rmat[1, 192:256, :], rmat[2, 0:64, :], rmat[2, 64:128, :],
         rmat[2, 128:192, :]], 1)
    total = total + 0.5 * dot(ysum[:, 0:RANK].astype(BF16), ro)
    for n in range(1, CHIPS):
        src = (chip + n) % CHIPS
        pltpu.make_async_copy(crecv.at[src], crecv.at[src], crecv_sem.at[src]).wait()
        total = total + crecv[src].astype(F32)
    hid[zlo, :, pl.ds(pl.multiple_of(mine, 128), BLOCK)] = total.astype(BF16)

    def block(k, c):
        return hid.at[c // XS, :, pl.ds(pl.multiple_of(k * HALF + (c % XS) * BLOCK, 128), BLOCK)]

    def gcopy(c):
        return pltpu.make_async_remote_copy(
            block(core, chip), block(core, chip), gsend_sem.at[c], grecv_sem.at[chip],
            device_id={"tensor": 2 * c + core}, device_id_type=MESH)

    def fcopy(c):
        return pltpu.make_async_remote_copy(
            block(core, c), block(core, c), fsend_sem.at[c], frecv_sem.at[c],
            device_id={"tensor": sib}, device_id_type=MESH)

    peers(lambda c: gcopy(c).start())
    pend["G", "sent"] = lambda: peers(lambda c: gcopy(c).wait_send())
    fcopy(chip).start()
    pend["F0", "sent"] = lambda: fcopy(chip).wait_send()
    pend["F", "sent"] = lambda: peers(lambda c: fcopy(c).wait_send())
    for n in range(1, CHIPS):
        src = (chip + n) % CHIPS
        pltpu.make_async_copy(block(core, src), block(core, src), grecv_sem.at[src]).wait()
        fcopy(src).start()
    for n in range(CHIPS):
        c = (chip + n) % CHIPS
        pltpu.make_async_copy(block(other, c), block(other, c), frecv_sem.at[c]).wait()

    ready("pgain")
    sq = jnp.zeros((2, ROWS, 1), F32)
    for i in range(8):
        cols = slice(i * 640, (i + 1) * 640)
        v = hid[:, :, cols]
        hid_out[:, :, cols] = v
        v = v.astype(F32)
        sq = sq + jnp.sum(v * v, -1, keepdims=True)
    rs = lax.rsqrt(sq * (1.0 / WIDTH) + 1e-06)
    for i in range(8):
        cols = slice(i * 640, (i + 1) * 640)
        v = hid[:, :, cols].astype(F32) * rs * pgain[:, cols][None]
        mlp_out[:, :, cols] = v.astype(BF16)

    finish()


def close_kernel(hid_ref, mlp_ref, kv_ref, hid_out, mlp_out, kv_out, sems):
    copies = []
    for k, (src, dst) in enumerate(((hid_ref, hid_out), (mlp_ref, mlp_out), (kv_ref, kv_out))):
        copies.append(pltpu.make_async_copy(src, dst, sems.at[k]))
    for c in copies:
        c.start()
    for c in copies:
        c.wait()


def shards(
    tokens_in, attn_gain, post_gain, w_query, key_weight_base, value_weight_base, w_out, left_qkv,
    right_query, right_key_value, left_out, right_out, kv_cache, lengths, starts,
):
    hbm = pl.BlockSpec(memory_space=pltpu.HBM)
    vmem = pl.BlockSpec(memory_space=pltpu.VMEM)
    dma = pltpu.SemaphoreType.DMA
    scratch = [
        pltpu.VMEM((2, ROWS, WIDTH), BF16),
        pltpu.VMEM((1, WIDTH), F32),
        pltpu.VMEM((1, WIDTH), F32),
        pltpu.VMEM((WIDTH, 512), BF16),
        pltpu.VMEM((512, HALF), BF16),
        pltpu.VMEM((2, ROWS, SLOTS, HEAD), BF16),
        pltpu.VMEM((1, ROWS), jnp.int32),
        pltpu.VMEM((1, ROWS), jnp.int32),
        pltpu.VMEM((16, LROWS), F32),
        pltpu.VMEM((4, 256), F32),
        pltpu.VMEM((2, 4, 128), F32),
        pltpu.VMEM((4, 256), F32),
        pltpu.VMEM((4, BLOCK), F32),
        pltpu.VMEM((16, LPAD), BF16),
        pltpu.VMEM((DP, 16, LPAD), BF16),
        pltpu.VMEM((16, 128), BF16),
        pltpu.VMEM((32, 128), BF16),
        pltpu.VMEM((DP, 16, 128), BF16),
        pltpu.VMEM((DP, 32, 128), BF16),
        pltpu.VMEM((12, 16, 128), BF16),
        pltpu.VMEM((3, 256, 128), BF16),
        pltpu.VMEM((2, 128, 128), BF16),
        pltpu.VMEM((2 * ROWS, WIDTH), BF16),
        pltpu.VMEM((2 * ROWS, 512), F32),
        pltpu.VMEM((4 * ROWS, HEAD), F32),
        pltpu.VMEM((2, 4 * ROWS, HEAD), F32),
        pltpu.VMEM((2, 4 * ROWS, HEAD), F32),
        pltpu.VMEM((4 * ROWS, SLOTS), F32),
        pltpu.VMEM((4 * ROWS, SLOTS), BF16),
        pltpu.VMEM((4 * ROWS, HEAD), F32),
        pltpu.VMEM((2, 2 * ROWS, 256), BF16),
        pltpu.VMEM((2, ROWS, 128), BF16),
        pltpu.VMEM((CHIPS, ROWS, 128), BF16),
        pltpu.VMEM((CHIPS, ROWS, BLOCK), BF16),
        pltpu.VMEM((CHIPS, ROWS, BLOCK), BF16),
        pltpu.VMEM((2, ROWS, WIDTH), BF16),
        dma((32,)),
        dma((DP,)), dma((DP,)), dma((DP,)), dma((DP,)), dma((DP,)), dma((DP,)),
        dma((TP,)), dma((12,)), dma((3,)), dma((3,)),
        dma((CHIPS,)), dma((CHIPS,)), dma((CHIPS,)), dma((CHIPS,)),
        dma((CHIPS,)), dma((CHIPS,)), dma((CHIPS,)), dma((CHIPS,)),
    ]
    shapes = (
        jax.ShapeDtypeStruct((2, ROWS, WIDTH), BF16),
        jax.ShapeDtypeStruct((2, ROWS, WIDTH), BF16),
        jax.ShapeDtypeStruct((2, 2, ROWS, HEAD), BF16),
    )
    args = (
        tokens_in, attn_gain.reshape(1, WIDTH), post_gain.reshape(1, WIDTH), w_query,
        key_weight_base, value_weight_base, w_out, left_qkv.swapaxes(1, 2), right_query,
        right_key_value, left_out.T, right_out, kv_cache, lengths.reshape(1, ROWS),
        starts.reshape(1, ROWS),
    )
    results = pl.pallas_call(
        main_kernel,
        out_shape=tuple(pltpu.VMEM(s.shape, s.dtype) for s in shapes),
        in_specs=[hbm] * len(args),
        out_specs=(vmem, vmem, vmem),
        scratch_shapes=scratch,
        compiler_params=pltpu.CompilerParams(
            collective_id=0, has_side_effects=True, vmem_limit_bytes=40 * 1024 * 1024),
    )(*[pltpu.with_memory_space_constraint(a, pltpu.HBM) for a in args])
    return pl.pallas_call(
        close_kernel,
        out_shape=shapes,
        in_specs=[vmem] * 3,
        out_specs=(hbm, hbm, hbm),
        scratch_shapes=[dma((3,))],
    )(*[pltpu.with_memory_space_constraint(a, pltpu.VMEM) for a in results])


def solution(mesh):
    in_specs = (
        P(None, "dp", None),
        P(),
        P(),
        P(None, "tensor"),
        P(None, "tensor"),
        P(None, "tensor"),
        P("tensor", None),
        P(None, "dp", None),
        P("dp", "tensor"),
        P(None, "dp", "tensor"),
        P("tensor", "dp"),
        P("dp", None),
        P(None, "dp", "tensor", None, None),
        P("dp"),
        P("dp"),
    )
    out_specs = (P(None, "dp", None), P(None, "dp", None), P(None, None, "dp", "tensor"))
    return jax.shard_map(shards, mesh=mesh, in_specs=in_specs, out_specs=out_specs, check_vma=False)
```

```python
import math

import jax
import jax.numpy as jnp
from jax import lax
from jax.experimental import pallas as pl
from jax.experimental.pallas import tpu as pltpu
from jax.sharding import PartitionSpec as P

MESH = pl.DeviceIdType.MESH
BF16 = jnp.bfloat16
F32 = jnp.float32

WIDTH = 5120
HEAD = 128
SLOTS = 320
WINDOW = 256
RANK = 64
ROWS = 24
DP = 16
TP = 16
CHIPS = 8
XS = 4
HALF = WIDTH // 2
BLOCK = HALF // XS
PARTS = ((0, 256), (256, 384))
LROWS = WIDTH // DP
LPAD = 384
NT = (((1,), (1,)), ((), ()))
TN = (((0,), (0,)), ((), ()))
NN = (((1,), (0,)), ((), ()))


def dot(a, b, dims=NN):
    return lax.dot_general(a, b, dims, preferred_element_type=F32)


def iota(shape, axis):
    return lax.broadcasted_iota(jnp.int32, shape, axis)


def one_hot(cond):
    return jnp.where(cond, 1.0, 0.0).astype(BF16)


def main_kernel(
    tok_in, gain_in, pgain_in, wq_in, wk_in, wv_in, wo_in, lqkv_in, rq_in, rkv_in, lo_in, ro_in,
    kv_in, len_in, start_in,
    hid_out, mlp_out, kv_out,
    tok, gain, pgain, w, wo, kvc, lens, starts,
    lbuf, rq, rkv, lob, rob,
    lsend, lgat, pagat, pbgat, zgat, rbig, rmat, losib,
    normed, proj, qs, kx, vx, score, prob, att, attboth, keep, ysend, yall, csa, csb, cra, crb,
    loc, lsend_sem, lrecv_sem, asend_sem, arecv_sem, psend_sem, precv_sem, zsend_sem, zrecv_sem,
    sib_send, sib_recv, ysend_sem, yrecv_sem, csend_sem, crecv_sem,
    gsend_sem, grecv_sem, fsend_sem, frecv_sem,
):
    dp = lax.axis_index("dp")
    tp = lax.axis_index("tensor")
    chip = tp // 2
    core = tp % 2
    zlo = chip // XS
    xpos = chip % XS
    yrow = dp // 4
    zhi = dp % 4
    lane8 = tp % 8
    sib = tp + 1 - 2 * core
    other = 1 - core
    ys = [(yrow + d) % 4 * 4 for d in range(4)]
    zs = [(zhi + d) % 4 for d in range(4)]
    xs = [(xpos + d) % XS for d in range(XS)]
    zlos = [zlo, 1 - zlo]
    cores = [core, other]
    zstep = jnp.where(zlo == 0, zs[3], zs[1])
    pend = {}

    def finish():
        for wait in pend.values():
            wait()

    barrier = pltpu.get_barrier_semaphore()

    def greet(device):
        pl.semaphore_signal(barrier, inc=1, device_id=device, device_id_type=MESH)

    for dz, copy_at in ((2, zlos[1]), (1, 0), (3, 1), (0, zlo)):
        for dy in (2, 1, 3, 0):
            if dz or dy:
                greet({"dp": ys[dy] + zs[dz], "tensor": copy_at * 8 + lane8})
    for dz in (2, 1, 3):
        greet({"dp": ys[0] + zs[dz]})
    group = [(z, x, c) for x in (2, 1, 3, 0) for z in (1, 0) for c in (0, 1)][:-2]
    group = [p for p in group if any(p)] + [(0, 0, 1)]

    def member(p):
        return zlos[p[0]] * 8 + xs[p[1]] * 2 + cores[p[2]]

    for p in group:
        greet({"tensor": member(p)})

    def load(name, src, dst):
        c = pltpu.make_async_copy(src, dst, loc.at[len(pend)])
        c.start()
        pend[name] = c.wait

    def ready(*names):
        for name in names:
            pend.pop(name)()

    active = jnp.logical_or(zlo == 0, core == 0)
    slab = jnp.where(zlo == 0, lane8, 8 + lane8 // 2)
    mine = core * HALF + xpos * BLOCK
    rows = pl.ds(pl.multiple_of(16 * (lane8 % 4), 16), 16)
    load("l0", lqkv_in.at[lane8 // 4, rows], lbuf.at[0])
    load("l1", lqkv_in.at[2, pl.ds(pl.multiple_of(16 * (lane8 // 2), 16), 16)], lbuf.at[1])
    load("rq", rq_in, rq)
    load("rkv", rkv_in, rkv)
    load("lo", lo_in, lob)
    load("ro", ro_in.at[:, pl.ds(pl.multiple_of(mine, 128), BLOCK)], rob)
    load("tok", tok_in, tok)
    load("gain", gain_in, gain)
    load("len", len_in, lens)
    load("start", start_in, starts)
    step = WIDTH // 4
    for i in range(4):
        rs = pl.ds(i * step, step)
        load(("wq", i), wq_in.at[rs], w.at[rs, 0:256])
        load(("wk", i), wk_in.at[rs], w.at[rs, 256:384])
        load(("wv", i), wv_in.at[rs], w.at[rs, 384:512])
    load("k", kv_in.at[0, :, 0], kvc.at[0])
    load("v", kv_in.at[1, :, 0], kvc.at[1])
    load("wo", wo_in.at[:, pl.ds(pl.multiple_of(core * HALF, 128), HALF)], wo.at[0:256])
    load("pgain", pgain_in, pgain)

    ready("l0", "l1")
    for k in range(2):
        rank_rows = jnp.concatenate([lbuf[k], jnp.zeros((16, LPAD - LROWS), F32)], 1)
        rank_rows = jnp.where(dp % 2 == 1, pltpu.roll(rank_rows, LPAD - LROWS, 1), rank_rows)
        lsend[k] = rank_rows.astype(BF16)
    lgat[dp] = lsend[zlo]

    pl.semaphore_wait(barrier, 15 + 15 + 3)

    def each_l(f):
        def to(k, dy, dp_z, to_zlo):
            if k or dy:
                f(pltpu.make_async_remote_copy(
                    lsend.at[to_zlo], lgat.at[dp], lsend_sem.at[4 * k + dy], lrecv_sem.at[dp],
                    device_id={"dp": ys[dy] + dp_z, "tensor": to_zlo * 8 + lane8},
                    device_id_type=MESH))

        @pl.when(jnp.logical_or(zlo == 1, core == 0))
        def _():
            for k, z in ((3, zs[2]), (2, zstep)):
                for dy in (2, 1, 3, 0):
                    to(k, dy, z, zlos[1])

        @pl.when(active)
        def _():
            for k, z in ((1, zstep), (0, zhi)):
                for dy in (2, 1, 3, 0):
                    to(k, dy, z, zlo)

    def got_l():
        @pl.when(active)
        def _():
            for dz in (0, 1, 3, 2):
                for dy in (0, 1, 3, 2):
                    if dz or dy:
                        who = ys[dy] + zs[dz]
                        pltpu.make_async_copy(lgat.at[who], lgat.at[who], lrecv_sem.at[who]).wait()

    each_l(lambda c: c.start())
    pend["L", "sent"] = lambda: each_l(lambda c: c.wait_send())
    pend["L"] = got_l

    def ring(name, buf, send, recv, along_y):
        copies, waits = [], []
        for d in range(1, 4):
            if along_y:
                to = ys[d] + zhi
                src, came = buf.at[pl.ds(ys[0], 4)], buf.at[pl.ds(ys[4 - d], 4)]
            else:
                to = ys[0] + zs[d]
                src, came = buf.at[dp], buf.at[ys[0] + zs[4 - d]]
            k = d + 4 * along_y
            c = pltpu.make_async_remote_copy(
                src, src, send.at[k], recv.at[k], device_id={"dp": to}, device_id_type=MESH)
            copies.append(c)
            waits.append(pltpu.make_async_copy(came, came, recv.at[k]))
        for d in (2, 1, 3):
            copies[d - 1].start()
        pend[name, "sent"] = lambda: [c.wait_send() for c in copies]
        pend[name] = lambda: [c.wait() for c in waits]

    def when_active(f):
        @pl.when(active)
        def _():
            f()

    ready("rq", "rkv")
    tiles = [rq[:, 0:128], rq[:, 128:256], rkv[0], rkv[1]]
    pagat[dp] = jnp.concatenate(tiles, 0).astype(BF16)
    ring("Az", pagat, asend_sem, arecv_sem, False)
    ready("lo", "ro")
    tiles = [lob[:, 0:128], lob[:, 128:256]]
    tiles += [rob[:, 128 * i : 128 * (i + 1)] for i in range(5)]
    tiles += [jnp.zeros((4, 128), F32)]
    pbgat[dp] = jnp.concatenate(tiles, 0).astype(BF16)
    ring("Bz", pbgat, psend_sem, precv_sem, False)

    def to_sib(src, dst, k, name):
        c = pltpu.make_async_remote_copy(
            src, dst, sib_send.at[k], sib_recv.at[k],
            device_id={"tensor": sib}, device_id_type=MESH)
        c.start()
        pend[name, "sent"] = c.wait_send
        pend[name] = c.wait_recv

    to_sib(wo_in.at[:, pl.ds(pl.multiple_of(other * HALF, 128), HALF)], wo.at[256:512], 0, "wosib")


    ready("tok", "gain")
    sq = jnp.zeros((2, ROWS, 1), F32)
    for i in range(8):
        v = tok[:, :, i * 640 : (i + 1) * 640].astype(F32)
        sq = sq + jnp.sum(v * v, -1, keepdims=True)
    rs = lax.rsqrt(sq * (1.0 / WIDTH) + 1e-06)
    for i in range(8):
        cols = slice(i * 640, (i + 1) * 640)
        v = tok[:, :, cols].astype(F32) * rs * gain[:, cols][None]
        normed[:, cols] = v.reshape(2 * ROWS, 640).astype(BF16)

    acc = None
    for i in range(2):
        ready(("wq", i), ("wk", i), ("wv", i))
        part = dot(normed[:, i * step : (i + 1) * step], w[i * step : (i + 1) * step, :])
        acc = part if acc is None else acc + part
    proj[...] = acc

    ready("Az")
    ring("A", pagat, asend_sem, arecv_sem, True)
    ready("L")

    def zcopy(k):
        return pltpu.make_async_remote_copy(
            zgat.at[slab], zgat.at[slab], zsend_sem.at[k], zrecv_sem.at[slab],
            device_id={"tensor": member(group[k])}, device_id_type=MESH)

    @pl.when(active)
    def _():
        parts = []
        for j in range(0, DP, 2):
            parts += [lgat[j, :, 0:256], lgat[j, :, 256:384] + lgat[j + 1, :, 0:128]]
            parts += [lgat[j + 1, :, 128:384]]
        z = dot(jnp.concatenate(parts, 1), normed[...], NT)
        z = jnp.concatenate([z, jnp.zeros((16, 128 - 2 * ROWS), F32)], 1)
        zgat[slab] = z.astype(BF16)

        for k in range(TP - 1):
            zcopy(k).start()

    def sent_z():
        @pl.when(active)
        def _():
            for k in range(TP - 1):
                zcopy(k).wait_send()

    def got_z():
        def got(s, _):
            src = jnp.where(s < 8, s, 2 * s - 8)

            @pl.when(src != tp)
            def _():
                pltpu.make_async_copy(zgat.at[s], zgat.at[s], zrecv_sem.at[s]).wait()

            return 0

        lax.fori_loop(0, 12, got, 0)

    pend["Z", "sent"] = sent_z
    pend["Z"] = got_z
    ready("Bz")
    ring("B", pbgat, psend_sem, precv_sem, True)
    acc = proj[...]
    for i in range(2, 4):
        ready(("wq", i), ("wk", i), ("wv", i))
        acc = acc + dot(normed[:, i * step : (i + 1) * step], w[i * step : (i + 1) * step, :])
    proj[...] = acc

    ready("len", "start")
    lenf = lens[...].astype(F32)
    stf = starts[...].astype(F32)

    def column(values, rows, owner):
        hit = owner(iota((rows, ROWS), 0)) == iota((rows, ROWS), 1)
        return jnp.sum(jnp.where(hit, values, 0.0), -1, keepdims=True)

    row = iota((2 * ROWS, 1), 0)
    pos = column(lenf, 2 * ROWS, lambda r: r % ROWS) + jnp.where(row >= ROWS, 1.0, 0.0)
    lane = iota((1, HEAD), 1)
    freq = jnp.exp((lane % 64).astype(F32) * (-2.0 * math.log(1000000.0) / HEAD))
    angle = pos * freq
    cos = jnp.cos(angle)
    sin = jnp.sin(angle) * jnp.where(lane < 64, -1.0, 1.0)

    def rope(v):
        return v * cos + pltpu.roll(v, 64, 1) * sin

    arow = iota((4 * ROWS, 1), 0)
    tokstep = jnp.where(arow % 4 >= 2, 1.0, 0.0)
    alen = column(lenf, 4 * ROWS, lambda r: r // 4)
    ast = column(stf, 4 * ROWS, lambda r: r // 4)
    slot = iota((4 * ROWS, SLOTS), 1).astype(F32) - ast
    slot = jnp.where(slot < 0, slot + float(SLOTS), slot)
    visible = jnp.logical_and(slot < alen, alen + tokstep - slot < float(WINDOW))

    ready("A")
    o = iota((256, 256), 0)
    perm = one_hot(iota((256, 256), 1) == ((o % 64) // 4) * 16 + 4 * (o // 64) + o % 4)
    right = dot(perm, pagat[...].reshape(256, 128)).astype(BF16)
    rbig[...] = jnp.zeros_like(rbig)
    for t, p in enumerate((0, 0, 1, 2)):
        rbig[64 * p : 64 * (p + 1), 128 * t : 128 * (t + 1)] = right[64 * t : 64 * (t + 1)]

    ready(("L", "sent"), ("Az", "sent"), ("wosib", "sent"))
    ready("Z")
    delta = dot(zgat[...].reshape(3 * RANK, 128), rbig[...], TN)[: 2 * ROWS]
    delta = proj[...] + 0.5 * delta
    cols = [delta[:, 128 * t : 128 * (t + 1)] for t in range(4)]
    rounded = [rope(cols[0]), rope(cols[1]), rope(cols[2]), cols[3]]
    rounded = [v.astype(BF16).astype(F32) for v in rounded]
    for t in range(2):
        rows = slice(t * ROWS, (t + 1) * ROWS)
        kv_out[t, 0] = rounded[2][rows].astype(BF16)
        kv_out[t, 1] = rounded[3][rows].astype(BF16)
        for g in range(2):
            qs[pl.ds(2 * t + g, ROWS, stride=4), :] = rounded[g][rows]
        for r in range(4):
            kx[t, pl.ds(r, ROWS, stride=4), :] = rounded[2][rows]
            vx[t, pl.ds(r, ROWS, stride=4), :] = rounded[3][rows]

    scale = 1.0 / math.sqrt(HEAD)
    ready("k")
    which = iota((16, 1), 0) // 4
    odd = which % 2 == 1
    for i in range(6):
        q = qs[16 * i : 16 * (i + 1), :]
        q = jnp.concatenate([jnp.where(odd, 0.0, q), jnp.where(odd, q, 0.0)], 1).astype(BF16)
        k = [jnp.concatenate([kvc[0, 4 * i + b], kvc[0, 4 * i + b + 1]], 1) for b in (0, 2)]
        score[16 * i : 16 * (i + 1), :] = jnp.where(which < 2, dot(q, k[0], NT), dot(q, k[1], NT))
    sc = jnp.where(visible, score[...] * scale, -1e30)
    q = qs[...]
    f0 = jnp.sum(q * kx[0], -1, keepdims=True) * scale
    f1 = jnp.sum(q * kx[1], -1, keepdims=True) * scale
    f1 = jnp.where(tokstep > 0.5, f1, -1e30)
    top = jnp.maximum(jnp.max(sc, -1, keepdims=True), jnp.maximum(f0, f1))
    ex = jnp.exp(sc - top)
    e0 = jnp.exp(f0 - top)
    e1 = jnp.exp(f1 - top)
    den = jnp.sum(ex, -1, keepdims=True) + (e0 + e1)
    prob[...] = (ex / den).astype(BF16)
    p0 = (e0 / den).astype(BF16).astype(F32)
    p1 = (e1 / den).astype(BF16).astype(F32)
    att[...] = p0 * vx[0] + p1 * vx[1]
    ready("v")
    for i in range(6):
        rows = slice(16 * i, 16 * (i + 1))
        p = prob[rows, :]
        v = [jnp.concatenate([kvc[1, 4 * i + b], kvc[1, 4 * i + b + 1]], 1) for b in (0, 2)]
        s = jnp.where(which < 2, dot(p, v[0]), dot(p, v[1]))
        att[rows, :] = att[rows, :] + jnp.where(odd, s[:, 128:256], s[:, 0:128])
    heads = []
    for g in range(2):
        heads.append(jnp.concatenate([att[pl.ds(2 * t + g, ROWS, stride=4), :] for t in range(2)], 0))
    attboth[0] = jnp.concatenate(heads, 1).astype(BF16)

    to_sib(attboth.at[0], attboth.at[1], 1, "att")
    ready("B")
    grp = pbgat[:, 0:16, :].reshape(256, 128)
    rmat[0] = dot(perm, grp).astype(BF16)
    losib[0] = rmat[0, 0:128, :]
    to_sib(losib.at[0], losib.at[1], 2, "losib")
    grp = pbgat[:, 16:32, :].reshape(256, 128)
    rmat[1] = dot(perm, grp).astype(BF16)

    offsets = ((1, 2), (0, 2), (1, 1), (1, 3), (0, 1), (0, 3), (1, 0))

    def at(o):
        return zlos[o[0]] * XS + xs[o[1]]

    def source(o):
        return zlos[o[0]] * XS + xs[-o[1]]

    def ccopy(c, h):
        send, recv = (csa, cra) if h == 0 else (csb, crb)
        return pltpu.make_async_remote_copy(
            send.at[c], recv.at[chip], csend_sem.at[h, c], crecv_sem.at[h, chip],
            device_id={"tensor": 2 * c + core}, device_id_type=MESH)

    def ycopy(c):
        return pltpu.make_async_remote_copy(
            ysend.at[c // XS], yall.at[chip], ysend_sem.at[c], yrecv_sem.at[chip],
            device_id={"tensor": 2 * c + core}, device_id_type=MESH)

    ready("wo")
    own = attboth[0]
    for h, (first, width) in enumerate(PARTS):
        for n in (2, 1, 3, 0):
            cols = pl.ds(pl.multiple_of(xs[n] * BLOCK + first, 128), width)
            keep[n, :, first : first + width] = dot(own, wo[0:256, cols])
    ready("wosib", "att")
    theirs = attboth[1]
    total = []
    for h, (first, width) in enumerate(PARTS):
        for n in (2, 1, 3, 0):
            x = xs[n]
            cols = pl.ds(pl.multiple_of(x * BLOCK + first, 128), width)
            part = keep[n, :, first : first + width] + dot(theirs, wo[256:512, cols])
            for t in range(2):
                (csa, csb)[h][t * XS + x] = part[t * ROWS : (t + 1) * ROWS].astype(BF16)
            ccopy(zlos[1] * XS + x, h).start()
            if n != 0:
                ccopy(zlo * XS + x, h).start()
            else:
                total.append(jnp.where(zlo == 0, part[0:ROWS], part[ROWS:]))
        if h == 0:
            ready("losib")
            lot = [jnp.concatenate([losib[k, 0:64], losib[k, 64:128]], 1) for k in range(2)]
            y = dot(own, lot[0], NT) + dot(theirs, lot[1], NT)
            y = jnp.concatenate([y, jnp.zeros((2 * ROWS, 128 - RANK), F32)], 1)
            ysend[0] = y[0:ROWS].astype(BF16)
            ysend[1] = y[ROWS:].astype(BF16)
            for o in offsets:
                ycopy(at(o)).start()
    pend["Y", "sent"] = lambda: [ycopy(at(o)).wait_send() for o in offsets]
    pend["C", "sent"] = lambda: [ccopy(at(o), h).wait_send() for o in offsets for h in range(2)]

    ready(("A", "sent"), ("Bz", "sent"), ("B", "sent"), ("Z", "sent"), ("att", "sent"))
    ready(("losib", "sent"))
    ysum = jnp.where(zlo == 0, y[0:ROWS], y[ROWS:])
    for o in offsets[::-1]:
        src = source(o)
        pltpu.make_async_copy(yall.at[src], yall.at[src], yrecv_sem.at[src]).wait()
        ysum = ysum + yall[src].astype(F32)
    ysum = (0.5 * ysum[:, 0:RANK]).astype(BF16)
    ro = jnp.concatenate(
        [rmat[0, 128:192, :], rmat[0, 192:256, :], rmat[1, 0:64, :], rmat[1, 64:128, :],
         rmat[1, 128:192, :]], 1)

    def block(k, c, h):
        return hid_out.at[c // XS, :, pl.ds(
            pl.multiple_of(k * HALF + c % XS * BLOCK + PARTS[h][0], 128), PARTS[h][1])]

    def gcopy(c, h):
        return pltpu.make_async_remote_copy(
            block(core, chip, h), block(core, chip, h), gsend_sem.at[h, c], grecv_sem.at[h, chip],
            device_id={"tensor": 2 * c + core}, device_id_type=MESH)

    def fcopy(c, h):
        return pltpu.make_async_remote_copy(
            block(core, c, h), block(core, c, h), fsend_sem.at[h, c], frecv_sem.at[h, c],
            device_id={"tensor": sib}, device_id_type=MESH)

    def squares(v):
        v = v.astype(F32)
        v = v * v
        return sum(v[:, i : i + 128] for i in range(0, v.shape[1], 128))

    sq = [jnp.zeros((ROWS, 128), F32) for _ in range(2)]
    for h, (first, width) in enumerate(PARTS):
        here = pl.ds(pl.multiple_of(mine + first, 128), width)
        out = total[h] + tok[zlo, :, here].astype(F32) + dot(ysum, ro[:, first : first + width])
        recv = (cra, crb)[h]
        for o in offsets[::-1]:
            src = source(o)
            pltpu.make_async_copy(recv.at[src], recv.at[src], crecv_sem.at[h, src]).wait()
            out = out + recv[src].astype(F32)
        out = out.astype(BF16)
        hid_out[zlo, :, here] = out
        sq[0] = sq[0] + squares(out)
        for o in offsets:
            gcopy(at(o), h).start()
        fcopy(chip, h).start()
    pend["G", "sent"] = lambda: [gcopy(at(o), h).wait_send() for o in offsets for h in range(2)]
    every = ((0, 0),) + offsets[::-1]
    ready(("Y", "sent"), ("C", "sent"))
    pend["F", "sent"] = lambda: [fcopy(source(o), h).wait_send() for o in every for h in range(2)]
    for h in range(2):
        for o in offsets[::-1]:
            mark = block(core, source(o), h)
            pltpu.make_async_copy(mark, mark, grecv_sem.at[h, source(o)]).wait()
            fcopy(source(o), h).start()
            sq[o[0]] = sq[o[0]] + squares(mark[...])
    ready(("G", "sent"))
    for h in range(2):
        for o in every:
            mark = block(other, source(o), h)
            pltpu.make_async_copy(mark, mark, frecv_sem.at[h, source(o)]).wait()
            sq[o[0]] = sq[o[0]] + squares(mark[...])

    ready("pgain")
    for t in range(2):
        mean = jnp.sum(jnp.where(zlo == t, sq[0], sq[1]), -1, keepdims=True) * (1.0 / WIDTH)
        rs = lax.rsqrt(mean + 1e-06)
        for i in range(8):
            cols = slice(i * 640, (i + 1) * 640)
            mlp_out[t, :, cols] = (hid_out[t, :, cols].astype(F32) * rs * pgain[:, cols]).astype(BF16)

    finish()


def close_kernel(hid_ref, mlp_ref, kv_ref, hid_out, mlp_out, kv_out, sems):
    copies = []
    for k, (src, dst) in enumerate(((hid_ref, hid_out), (mlp_ref, mlp_out), (kv_ref, kv_out))):
        copies.append(pltpu.make_async_copy(src, dst, sems.at[k]))
    for c in copies:
        c.start()
    for c in copies:
        c.wait()


def shards(
    tokens_in, attn_gain, post_gain, w_query, key_weight_base, value_weight_base, w_out, left_qkv,
    right_query, right_key_value, left_out, right_out, kv_cache, lengths, starts,
):
    hbm = pl.BlockSpec(memory_space=pltpu.HBM)
    vmem = pl.BlockSpec(memory_space=pltpu.VMEM)
    dma = pltpu.SemaphoreType.DMA
    scratch = [
        pltpu.VMEM((2, ROWS, WIDTH), BF16),
        pltpu.VMEM((1, WIDTH), F32),
        pltpu.VMEM((1, WIDTH), F32),
        pltpu.VMEM((WIDTH, 512), BF16),
        pltpu.VMEM((512, HALF), BF16),
        pltpu.VMEM((2, ROWS, SLOTS, HEAD), BF16),
        pltpu.VMEM((1, ROWS), jnp.int32),
        pltpu.VMEM((1, ROWS), jnp.int32),
        pltpu.VMEM((2, 16, LROWS), F32),
        pltpu.VMEM((4, 256), F32),
        pltpu.VMEM((2, 4, 128), F32),
        pltpu.VMEM((4, 256), F32),
        pltpu.VMEM((4, BLOCK), F32),
        pltpu.VMEM((2, 16, LPAD), BF16),
        pltpu.VMEM((DP, 16, LPAD), BF16),
        pltpu.VMEM((DP, 16, 128), BF16),
        pltpu.VMEM((DP, 32, 128), BF16),
        pltpu.VMEM((12, 16, 128), BF16),
        pltpu.VMEM((3 * RANK, 512), BF16),
        pltpu.VMEM((2, 256, 128), BF16),
        pltpu.VMEM((2, 128, 128), BF16),
        pltpu.VMEM((2 * ROWS, WIDTH), BF16),
        pltpu.VMEM((2 * ROWS, 512), F32),
        pltpu.VMEM((4 * ROWS, HEAD), F32),
        pltpu.VMEM((2, 4 * ROWS, HEAD), F32),
        pltpu.VMEM((2, 4 * ROWS, HEAD), F32),
        pltpu.VMEM((4 * ROWS, SLOTS), F32),
        pltpu.VMEM((4 * ROWS, SLOTS), BF16),
        pltpu.VMEM((4 * ROWS, HEAD), F32),
        pltpu.VMEM((2, 2 * ROWS, 256), BF16),
        pltpu.VMEM((XS, 2 * ROWS, BLOCK), F32),
        pltpu.VMEM((2, ROWS, 128), BF16),
        pltpu.VMEM((CHIPS, ROWS, 128), BF16),
        pltpu.VMEM((CHIPS, ROWS, PARTS[0][1]), BF16),
        pltpu.VMEM((CHIPS, ROWS, PARTS[1][1]), BF16),
        pltpu.VMEM((CHIPS, ROWS, PARTS[0][1]), BF16),
        pltpu.VMEM((CHIPS, ROWS, PARTS[1][1]), BF16),
        dma((32,)),
        dma((DP,)), dma((DP,)), dma((8,)), dma((8,)), dma((8,)), dma((8,)),
        dma((TP,)), dma((12,)), dma((3,)), dma((3,)),
        dma((CHIPS,)), dma((CHIPS,)), dma((2, CHIPS)), dma((2, CHIPS)),
        dma((2, CHIPS)), dma((2, CHIPS)), dma((2, CHIPS)), dma((2, CHIPS)),
    ]
    shapes = (
        jax.ShapeDtypeStruct((2, ROWS, WIDTH), BF16),
        jax.ShapeDtypeStruct((2, ROWS, WIDTH), BF16),
        jax.ShapeDtypeStruct((2, 2, ROWS, HEAD), BF16),
    )
    args = (
        tokens_in, attn_gain.reshape(1, WIDTH), post_gain.reshape(1, WIDTH), w_query,
        key_weight_base, value_weight_base, w_out, left_qkv.swapaxes(1, 2), right_query,
        right_key_value, left_out.T, right_out, kv_cache, lengths.reshape(1, ROWS),
        starts.reshape(1, ROWS),
    )
    results = pl.pallas_call(
        main_kernel,
        out_shape=tuple(pltpu.VMEM(s.shape, s.dtype) for s in shapes),
        in_specs=[hbm] * len(args),
        out_specs=(vmem, vmem, vmem),
        scratch_shapes=scratch,
        compiler_params=pltpu.CompilerParams(
            collective_id=0, has_side_effects=True, vmem_limit_bytes=40 * 1024 * 1024),
    )(*[pltpu.with_memory_space_constraint(a, pltpu.HBM) for a in args])
    return pl.pallas_call(
        close_kernel,
        out_shape=shapes,
        in_specs=[vmem] * 3,
        out_specs=(hbm, hbm, hbm),
        scratch_shapes=[dma((3,))],
    )(*[pltpu.with_memory_space_constraint(a, pltpu.VMEM) for a in results])


def solution(mesh):
    in_specs = (
        P(None, "dp", None),
        P(),
        P(),
        P(None, "tensor"),
        P(None, "tensor"),
        P(None, "tensor"),
        P("tensor", None),
        P(None, "dp", None),
        P("dp", "tensor"),
        P(None, "dp", "tensor"),
        P("tensor", "dp"),
        P("dp", None),
        P(None, "dp", "tensor", None, None),
        P("dp"),
        P("dp"),
    )
    out_specs = (P(None, "dp", None), P(None, "dp", None), P(None, None, "dp", "tensor"))
    return jax.shard_map(shards, mesh=mesh, in_specs=in_specs, out_specs=out_specs, check_vma=False)
```

```python
import math

import jax
import jax.numpy as jnp
from jax import lax
from jax.experimental import pallas as pl
from jax.experimental.pallas import tpu as pltpu
from jax.sharding import PartitionSpec as P

MESH = pl.DeviceIdType.MESH
BF16 = jnp.bfloat16
F32 = jnp.float32

WIDTH = 5120
HEAD = 128
SLOTS = 320
WINDOW = 256
RANK = 64
ROWS = 24
DP = 16
TP = 16
CHIPS = 8
XS = 4
HALF = WIDTH // 2
BLOCK = HALF // XS
PARTS = ((0, 384), (384, 256))
LROWS = WIDTH // DP
LPAD = 384
NT = (((1,), (1,)), ((), ()))
TN = (((0,), (0,)), ((), ()))
NN = (((1,), (0,)), ((), ()))


def dot(a, b, dims=NN):
    return lax.dot_general(a, b, dims, preferred_element_type=F32)


def iota(shape, axis):
    return lax.broadcasted_iota(jnp.int32, shape, axis)


def one_hot(cond):
    return jnp.where(cond, 1.0, 0.0).astype(BF16)


def main_kernel(
    tok_in, gain_in, pgain_in, wq_in, wk_in, wv_in, wo_in, lqkv_in, rq_in, rkv_in, lo_in, ro_in,
    kv_in, len_in, start_in,
    hid_out, sq_out, pgain, kv_out,
    tok, gain, w, wo, kvc, lens, starts,
    lbuf, rq, rkv, lob, rob,
    lsend, lgat, pagat, pbgat, zgat, rbig, rmat,
    normed, proj, qs, kx, vx, score, prob, att, attboth, keep, ysend, yall, csend, crecv,
    loc, lsend_sem, lrecv_sem, asend_sem, arecv_sem, psend_sem, precv_sem, zsend_sem, zrecv_sem,
    sib_send, sib_recv, ysend_sem, yrecv_sem, csend_sem, crecv_sem,
    gsend_sem, grecv_sem, fsend_sem, frecv_sem,
):
    dp = lax.axis_index("dp")
    tp = lax.axis_index("tensor")
    chip = tp // 2
    core = tp % 2
    zlo = chip // XS
    xpos = chip % XS
    yrow = dp // 4
    zhi = dp % 4
    lane8 = tp % 8
    sib = tp + 1 - 2 * core
    other = 1 - core
    ys = [(yrow + d) % 4 * 4 for d in range(4)]
    zs = [(zhi + d) % 4 for d in range(4)]
    xs = [(xpos + d) % XS for d in range(XS)]
    zlos = [zlo, 1 - zlo]
    cores = [core, other]
    zstep = jnp.where(zlo == 0, zs[3], zs[1])
    pend = {}

    def finish():
        for wait in pend.values():
            wait()

    barrier = pltpu.get_barrier_semaphore()

    def greet(device):
        pl.semaphore_signal(barrier, inc=1, device_id=device, device_id_type=MESH)

    for dz, copy_at in ((2, zlos[1]), (1, 0), (3, 1), (0, zlo)):
        for dy in (2, 1, 3, 0):
            if dz or dy:
                greet({"dp": ys[dy] + zs[dz], "tensor": copy_at * 8 + lane8})
    for dz in (2, 1, 3):
        greet({"dp": ys[0] + zs[dz]})
    group = [(z, x, c) for x in (2, 1, 3, 0) for z in (1, 0) for c in (0, 1)][:-2]
    group = [p for p in group if any(p)] + [(0, 0, 1)]

    def member(p):
        return zlos[p[0]] * 8 + xs[p[1]] * 2 + cores[p[2]]

    for p in group:
        greet({"tensor": member(p)})

    def load(name, src, dst):
        c = pltpu.make_async_copy(src, dst, loc.at[len(pend)])
        c.start()
        pend[name] = c.wait

    def ready(*names):
        for name in names:
            pend.pop(name)()

    active = jnp.logical_or(zlo == 0, core == 0)
    slab = jnp.where(zlo == 0, lane8, 8 + lane8 // 2)
    mine = core * HALF + xpos * BLOCK
    rows = pl.ds(pl.multiple_of(16 * (lane8 % 4), 16), 16)
    load("l0", lqkv_in.at[lane8 // 4, rows], lbuf.at[0])
    load("l1", lqkv_in.at[2, pl.ds(pl.multiple_of(16 * (lane8 // 2), 16), 16)], lbuf.at[1])
    load("rq", rq_in, rq)
    load("rkv", rkv_in, rkv)
    load("lo", lo_in, lob)
    load("ro", ro_in.at[:, pl.ds(pl.multiple_of(mine, 128), BLOCK)], rob)
    load("tok", tok_in, tok)
    load("gain", gain_in, gain)
    load("len", len_in, lens)
    load("start", start_in, starts)
    step = WIDTH // 4
    for i in range(4):
        rs = pl.ds(i * step, step)
        load(("wq", i), wq_in.at[rs], w.at[rs, 0:256])
        load(("wk", i), wk_in.at[rs], w.at[rs, 256:384])
        load(("wv", i), wv_in.at[rs], w.at[rs, 384:512])
    load("k", kv_in.at[0, :, 0], kvc.at[0])
    load("v", kv_in.at[1, :, 0], kvc.at[1])
    load("wo", wo_in.at[:, pl.ds(pl.multiple_of(core * HALF, 128), HALF)], wo.at[0:256])
    load("pgain", pgain_in, pgain)

    ready("l0", "l1")
    for k in range(2):
        rank_rows = jnp.concatenate([lbuf[k], jnp.zeros((16, LPAD - LROWS), F32)], 1)
        rank_rows = jnp.where(dp % 2 == 1, pltpu.roll(rank_rows, LPAD - LROWS, 1), rank_rows)
        lsend[k] = rank_rows.astype(BF16)
    lgat[dp] = lsend[zlo]

    pl.semaphore_wait(barrier, 15 + 15 + 3)

    def each_l(f):
        def to(k, dy, dp_z, to_zlo):
            if k or dy:
                f(pltpu.make_async_remote_copy(
                    lsend.at[to_zlo], lgat.at[dp], lsend_sem.at[4 * k + dy], lrecv_sem.at[dp],
                    device_id={"dp": ys[dy] + dp_z, "tensor": to_zlo * 8 + lane8},
                    device_id_type=MESH))

        @pl.when(jnp.logical_or(zlo == 1, core == 0))
        def _():
            for k, z in ((3, zs[2]), (2, zstep)):
                for dy in (2, 1, 3, 0):
                    to(k, dy, z, zlos[1])

        @pl.when(active)
        def _():
            for k, z in ((1, zstep), (0, zhi)):
                for dy in (2, 1, 3, 0):
                    to(k, dy, z, zlo)

    def got_l():
        @pl.when(active)
        def _():
            for dz in (0, 1, 3, 2):
                for dy in (0, 1, 3, 2):
                    if dz or dy:
                        who = ys[dy] + zs[dz]
                        pltpu.make_async_copy(lgat.at[who], lgat.at[who], lrecv_sem.at[who]).wait()

    each_l(lambda c: c.start())
    pend["L", "sent"] = lambda: each_l(lambda c: c.wait_send())
    pend["L"] = got_l

    def ring(name, buf, send, recv, along_y):
        copies, waits = [], []
        for d in range(1, 4):
            if along_y:
                to = ys[d] + zhi
                src, came = buf.at[pl.ds(ys[0], 4)], buf.at[pl.ds(ys[4 - d], 4)]
            else:
                to = ys[0] + zs[d]
                src, came = buf.at[dp], buf.at[ys[0] + zs[4 - d]]
            k = d + 4 * along_y
            c = pltpu.make_async_remote_copy(
                src, src, send.at[k], recv.at[k], device_id={"dp": to}, device_id_type=MESH)
            copies.append(c)
            waits.append(pltpu.make_async_copy(came, came, recv.at[k]))
        for d in (2, 1, 3):
            copies[d - 1].start()
        pend[name, "sent"] = lambda: [c.wait_send() for c in copies]
        pend[name] = lambda: [c.wait() for c in waits]

    def when_active(f):
        @pl.when(active)
        def _():
            f()

    ready("rq", "rkv")
    tiles = [rq[:, 0:128], rq[:, 128:256], rkv[0], rkv[1]]
    pagat[dp] = jnp.concatenate(tiles, 0).astype(BF16)
    ring("Az", pagat, asend_sem, arecv_sem, False)
    ready("lo", "ro")
    tiles = [lob[:, 0:128], lob[:, 128:256]]
    tiles += [rob[:, 128 * i : 128 * (i + 1)] for i in range(5)]
    tiles += [jnp.zeros((4, 128), F32)]
    pbgat[dp] = jnp.concatenate(tiles, 0).astype(BF16)
    ring("Bz", pbgat, psend_sem, precv_sem, False)

    def to_sib(src, dst, k, name):
        c = pltpu.make_async_remote_copy(
            src, dst, sib_send.at[k], sib_recv.at[k],
            device_id={"tensor": sib}, device_id_type=MESH)
        c.start()
        pend[name, "sent"] = c.wait_send
        pend[name] = c.wait_recv

    to_sib(wo_in.at[:, pl.ds(pl.multiple_of(other * HALF, 128), HALF)], wo.at[256:512], 0, "wosib")


    ready("tok", "gain")
    sq = jnp.zeros((2, ROWS, 1), F32)
    for i in range(8):
        v = tok[:, :, i * 640 : (i + 1) * 640].astype(F32)
        sq = sq + jnp.sum(v * v, -1, keepdims=True)
    rs = lax.rsqrt(sq * (1.0 / WIDTH) + 1e-06)
    for i in range(8):
        cols = slice(i * 640, (i + 1) * 640)
        v = tok[:, :, cols].astype(F32) * rs * gain[:, cols][None]
        normed[:, cols] = v.reshape(2 * ROWS, 640).astype(BF16)

    acc = None
    for i in range(2):
        ready(("wq", i), ("wk", i), ("wv", i))
        part = dot(normed[:, i * step : (i + 1) * step], w[i * step : (i + 1) * step, :])
        acc = part if acc is None else acc + part
    proj[...] = acc

    ready("Az")
    ring("A", pagat, asend_sem, arecv_sem, True)
    ready("L")

    def zcopy(k):
        return pltpu.make_async_remote_copy(
            zgat.at[slab], zgat.at[slab], zsend_sem.at[k], zrecv_sem.at[slab],
            device_id={"tensor": member(group[k])}, device_id_type=MESH)

    @pl.when(active)
    def _():
        parts = []
        for j in range(0, DP, 2):
            parts += [lgat[j, :, 0:256], lgat[j, :, 256:384] + lgat[j + 1, :, 0:128]]
            parts += [lgat[j + 1, :, 128:384]]
        z = dot(jnp.concatenate(parts, 1), normed[...], NT)
        z = jnp.concatenate([z, jnp.zeros((16, 128 - 2 * ROWS), F32)], 1)
        zgat[slab] = z.astype(BF16)

        for k in range(TP - 1):
            zcopy(k).start()

    def sent_z():
        @pl.when(active)
        def _():
            for k in range(TP - 1):
                zcopy(k).wait_send()

    def got_z():
        def got(s, _):
            src = jnp.where(s < 8, s, 2 * s - 8)

            @pl.when(src != tp)
            def _():
                pltpu.make_async_copy(zgat.at[s], zgat.at[s], zrecv_sem.at[s]).wait()

            return 0

        lax.fori_loop(0, 12, got, 0)

    pend["Z", "sent"] = sent_z
    pend["Z"] = got_z
    ready("Bz")
    ring("B", pbgat, psend_sem, precv_sem, True)
    acc = proj[...]
    for i in range(2, 4):
        ready(("wq", i), ("wk", i), ("wv", i))
        acc = acc + dot(normed[:, i * step : (i + 1) * step], w[i * step : (i + 1) * step, :])
    proj[...] = acc

    ready("len", "start")
    lenf = lens[...].astype(F32)
    stf = starts[...].astype(F32)

    def column(values, rows, owner):
        hit = owner(iota((rows, ROWS), 0)) == iota((rows, ROWS), 1)
        return jnp.sum(jnp.where(hit, values, 0.0), -1, keepdims=True)

    row = iota((2 * ROWS, 1), 0)
    pos = column(lenf, 2 * ROWS, lambda r: r % ROWS) + jnp.where(row >= ROWS, 1.0, 0.0)
    lane = iota((1, HEAD), 1)
    freq = jnp.exp((lane % 64).astype(F32) * (-2.0 * math.log(1000000.0) / HEAD))
    angle = pos * freq
    cos = jnp.cos(angle)
    sin = jnp.sin(angle) * jnp.where(lane < 64, -1.0, 1.0)

    def rope(v):
        return v * cos + pltpu.roll(v, 64, 1) * sin

    arow = iota((4 * ROWS, 1), 0)
    tokstep = jnp.where(arow % 4 >= 2, 1.0, 0.0)
    alen = column(lenf, 4 * ROWS, lambda r: r // 4)
    ast = column(stf, 4 * ROWS, lambda r: r // 4)
    slot = iota((4 * ROWS, SLOTS), 1).astype(F32) - ast
    slot = jnp.where(slot < 0, slot + float(SLOTS), slot)
    visible = jnp.logical_and(slot < alen, alen + tokstep - slot < float(WINDOW))

    ready("A")
    o = iota((256, 256), 0)
    perm = one_hot(iota((256, 256), 1) == ((o % 64) // 4) * 16 + 4 * (o // 64) + o % 4)
    right = dot(perm, pagat[...].reshape(256, 128)).astype(BF16)
    rbig[...] = jnp.zeros_like(rbig)
    for t, p in enumerate((0, 0, 1, 2)):
        rbig[64 * p : 64 * (p + 1), 128 * t : 128 * (t + 1)] = right[64 * t : 64 * (t + 1)]

    ready(("L", "sent"), ("Az", "sent"), ("wosib", "sent"))
    ready("Z")
    delta = dot(zgat[...].reshape(3 * RANK, 128), rbig[...], TN)[: 2 * ROWS]
    delta = proj[...] + 0.5 * delta
    cols = [delta[:, 128 * t : 128 * (t + 1)] for t in range(4)]
    rounded = [rope(cols[0]), rope(cols[1]), rope(cols[2]), cols[3]]
    rounded = [v.astype(BF16).astype(F32) for v in rounded]
    for t in range(2):
        rows = slice(t * ROWS, (t + 1) * ROWS)
        kv_out[t, 0] = rounded[2][rows].astype(BF16)
        kv_out[t, 1] = rounded[3][rows].astype(BF16)
        for g in range(2):
            qs[pl.ds(2 * t + g, ROWS, stride=4), :] = rounded[g][rows]
        for r in range(4):
            kx[t, pl.ds(r, ROWS, stride=4), :] = rounded[2][rows]
            vx[t, pl.ds(r, ROWS, stride=4), :] = rounded[3][rows]

    scale = 1.0 / math.sqrt(HEAD)
    ready("k")
    which = iota((16, 1), 0) // 4
    odd = which % 2 == 1
    for i in range(6):
        q = qs[16 * i : 16 * (i + 1), :]
        q = jnp.concatenate([jnp.where(odd, 0.0, q), jnp.where(odd, q, 0.0)], 1).astype(BF16)
        k = [jnp.concatenate([kvc[0, 4 * i + b], kvc[0, 4 * i + b + 1]], 1) for b in (0, 2)]
        score[16 * i : 16 * (i + 1), :] = jnp.where(which < 2, dot(q, k[0], NT), dot(q, k[1], NT))
    sc = jnp.where(visible, score[...] * scale, -1e30)
    q = qs[...]
    f0 = jnp.sum(q * kx[0], -1, keepdims=True) * scale
    f1 = jnp.sum(q * kx[1], -1, keepdims=True) * scale
    f1 = jnp.where(tokstep > 0.5, f1, -1e30)
    top = jnp.maximum(jnp.max(sc, -1, keepdims=True), jnp.maximum(f0, f1))
    ex = jnp.exp(sc - top)
    e0 = jnp.exp(f0 - top)
    e1 = jnp.exp(f1 - top)
    den = jnp.sum(ex, -1, keepdims=True) + (e0 + e1)
    prob[...] = (ex / den).astype(BF16)
    p0 = (e0 / den).astype(BF16).astype(F32)
    p1 = (e1 / den).astype(BF16).astype(F32)
    att[...] = p0 * vx[0] + p1 * vx[1]
    ready("v")
    for i in range(6):
        rows = slice(16 * i, 16 * (i + 1))
        p = prob[rows, :]
        v = [jnp.concatenate([kvc[1, 4 * i + b], kvc[1, 4 * i + b + 1]], 1) for b in (0, 2)]
        s = jnp.where(which < 2, dot(p, v[0]), dot(p, v[1]))
        att[rows, :] = att[rows, :] + jnp.where(odd, s[:, 128:256], s[:, 0:128])
    heads = []
    for g in range(2):
        heads.append(jnp.concatenate([att[pl.ds(2 * t + g, ROWS, stride=4), :] for t in range(2)], 0))
    attboth[0] = jnp.concatenate(heads, 1).astype(BF16)

    to_sib(attboth.at[0], attboth.at[1], 1, "att")
    own = attboth[0]
    ready("B")
    rmat[0] = dot(perm, pbgat[:, 0:16, :].reshape(256, 128)).astype(BF16)
    lot = jnp.concatenate([rmat[0, 0:64], rmat[0, 64:128]], 1)
    y = dot(own, lot, NT)
    y = jnp.concatenate([y, jnp.zeros((2 * ROWS, 128 - RANK), F32)], 1)
    ysend[0] = y[0:ROWS].astype(BF16)
    ysend[1] = y[ROWS:].astype(BF16)

    def ycopy(k):
        return pltpu.make_async_remote_copy(
            ysend.at[zlos[group[k][0]]], yall.at[tp], ysend_sem.at[k], yrecv_sem.at[tp],
            device_id={"tensor": member(group[k])}, device_id_type=MESH)

    for k in range(TP - 1):
        ycopy(k).start()
    pend["Y", "sent"] = lambda: [ycopy(k).wait_send() for k in range(TP - 1)]

    ready("wo")
    for n in (2, 1, 3, 0):
        cols = pl.ds(pl.multiple_of(xs[n] * BLOCK, 128), PARTS[0][1])
        keep[n] = dot(own, wo[0:256, cols])

    offsets = ((1, 2), (0, 2), (1, 1), (1, 3), (0, 1), (0, 3), (1, 0))

    def at(o):
        return zlos[o[0]] * XS + xs[o[1]]

    def source(o):
        return zlos[o[0]] * XS + xs[-o[1]]

    def ccopy(c, h):
        cols = pl.ds(*PARTS[h])
        return pltpu.make_async_remote_copy(
            csend.at[c, :, cols], crecv.at[chip, :, cols], csend_sem.at[h, c], crecv_sem.at[h, chip],
            device_id={"tensor": 2 * c + core}, device_id_type=MESH)

    ready("wosib", "att")
    theirs = attboth[1]
    both = jnp.concatenate([own, theirs], 1)
    total = []
    for h, (first, width) in enumerate(PARTS):
        for n in (2, 1, 3, 0):
            x = xs[n]
            cols = pl.ds(pl.multiple_of(x * BLOCK + first, 128), width)
            part = keep[n] + dot(theirs, wo[256:512, cols]) if h == 0 else dot(both, wo[:, cols])
            for t in range(2):
                csend[t * XS + x, :, first : first + width] = part[t * ROWS : (t + 1) * ROWS].astype(BF16)
            ccopy(zlos[1] * XS + x, h).start()
            if n != 0:
                ccopy(zlo * XS + x, h).start()
            else:
                total.append(jnp.where(zlo == 0, part[0:ROWS], part[ROWS:]))
    rmat[1] = dot(perm, pbgat[:, 16:32, :].reshape(256, 128)).astype(BF16)
    pend["C", "sent"] = lambda: [ccopy(at(o), h).wait_send() for o in offsets for h in range(len(PARTS))]

    ready(("A", "sent"), ("Bz", "sent"), ("B", "sent"), ("Z", "sent"), ("att", "sent"))
    ysum = jnp.where(zlo == 0, y[0:ROWS], y[ROWS:])
    for p in group[::-1]:
        src = member(p)
        pltpu.make_async_copy(yall.at[src], yall.at[src], yrecv_sem.at[src]).wait()
        ysum = ysum + yall[src].astype(F32)
    ysum = (0.5 * ysum[:, 0:RANK]).astype(BF16)
    ro = jnp.concatenate(
        [rmat[0, 128:192, :], rmat[0, 192:256, :], rmat[1, 0:64, :], rmat[1, 64:128, :],
         rmat[1, 128:192, :]], 1)

    def block(k, c, h):
        return hid_out.at[c // XS, :, pl.ds(
            pl.multiple_of(k * HALF + c % XS * BLOCK + PARTS[h][0], 128), PARTS[h][1])]

    def gcopy(c, h):
        return pltpu.make_async_remote_copy(
            block(core, chip, h), block(core, chip, h), gsend_sem.at[h, c], grecv_sem.at[h, chip],
            device_id={"tensor": 2 * c + core}, device_id_type=MESH)

    def fcopy(c, h):
        return pltpu.make_async_remote_copy(
            block(core, c, h), block(core, c, h), fsend_sem.at[h, c], frecv_sem.at[h, c],
            device_id={"tensor": sib}, device_id_type=MESH)

    def squares(v):
        v = v.astype(F32)
        v = v * v
        return sum(v[:, i : i + 128] for i in range(0, v.shape[1], 128))

    sq = [jnp.zeros((ROWS, 128), F32) for _ in range(2)]
    for h, (first, width) in enumerate(PARTS):
        here = pl.ds(pl.multiple_of(mine + first, 128), width)
        out = total[h] + tok[zlo, :, here].astype(F32) + dot(ysum, ro[:, first : first + width])
        cols = pl.ds(first, width)
        for o in offsets[::-1]:
            src = source(o)
            mark = crecv.at[src, :, cols]
            pltpu.make_async_copy(mark, mark, crecv_sem.at[h, src]).wait()
            out = out + mark[...].astype(F32)
        out = out.astype(BF16)
        hid_out[zlo, :, here] = out
        sq[0] = sq[0] + squares(out)
        for o in offsets:
            gcopy(at(o), h).start()
        fcopy(chip, h).start()
    pend["G", "sent"] = lambda: [gcopy(at(o), h).wait_send() for o in offsets for h in range(len(PARTS))]
    every = ((0, 0),) + offsets[::-1]
    ready(("Y", "sent"), ("C", "sent"))
    pend["F", "sent"] = lambda: [fcopy(source(o), h).wait_send() for o in every for h in range(len(PARTS))]
    for h in range(len(PARTS)):
        for o in offsets[::-1]:
            mark = block(core, source(o), h)
            pltpu.make_async_copy(mark, mark, grecv_sem.at[h, source(o)]).wait()
            fcopy(source(o), h).start()
            sq[o[0]] = sq[o[0]] + squares(mark[...])
    ready(("G", "sent"))
    for h in range(len(PARTS)):
        for o in every:
            mark = block(other, source(o), h)
            pltpu.make_async_copy(mark, mark, frecv_sem.at[h, source(o)]).wait()
            sq[o[0]] = sq[o[0]] + squares(mark[...])

    ready("pgain")
    for t in range(2):
        sq_out[t] = jnp.where(zlo == t, sq[0], sq[1])

    finish()


def close_kernel(hid, sq, gain, kv, hid_out, mlp_out, kv_out, mlp, sems):
    copies = []

    def send(src, dst):
        c = pltpu.make_async_copy(src, dst, sems.at[len(copies)])
        c.start()
        copies.append(c)

    send(hid, hid_out)
    send(kv, kv_out)
    for t in range(2):
        rs = lax.rsqrt(jnp.sum(sq[t], -1, keepdims=True) * (1.0 / WIDTH) + 1e-06)
        for half in range(2):
            for i in range(4 * half, 4 * half + 4):
                cols = slice(i * 640, (i + 1) * 640)
                mlp[t, :, cols] = (hid[t, :, cols].astype(F32) * rs * gain[:, cols]).astype(BF16)
            part = pl.ds(half * HALF, HALF)
            send(mlp.at[t, :, part], mlp_out.at[t, :, part])
    for c in copies:
        c.wait()


def shards(
    tokens_in, attn_gain, post_gain, w_query, key_weight_base, value_weight_base, w_out, left_qkv,
    right_query, right_key_value, left_out, right_out, kv_cache, lengths, starts,
):
    hbm = pl.BlockSpec(memory_space=pltpu.HBM)
    vmem = pl.BlockSpec(memory_space=pltpu.VMEM)
    dma = pltpu.SemaphoreType.DMA
    scratch = [
        pltpu.VMEM((2, ROWS, WIDTH), BF16),
        pltpu.VMEM((1, WIDTH), F32),
        pltpu.VMEM((WIDTH, 512), BF16),
        pltpu.VMEM((512, HALF), BF16),
        pltpu.VMEM((2, ROWS, SLOTS, HEAD), BF16),
        pltpu.VMEM((1, ROWS), jnp.int32),
        pltpu.VMEM((1, ROWS), jnp.int32),
        pltpu.VMEM((2, 16, LROWS), F32),
        pltpu.VMEM((4, 256), F32),
        pltpu.VMEM((2, 4, 128), F32),
        pltpu.VMEM((4, 256), F32),
        pltpu.VMEM((4, BLOCK), F32),
        pltpu.VMEM((2, 16, LPAD), BF16),
        pltpu.VMEM((DP, 16, LPAD), BF16),
        pltpu.VMEM((DP, 16, 128), BF16),
        pltpu.VMEM((DP, 32, 128), BF16),
        pltpu.VMEM((12, 16, 128), BF16),
        pltpu.VMEM((3 * RANK, 512), BF16),
        pltpu.VMEM((2, 256, 128), BF16),
        pltpu.VMEM((2 * ROWS, WIDTH), BF16),
        pltpu.VMEM((2 * ROWS, 512), F32),
        pltpu.VMEM((4 * ROWS, HEAD), F32),
        pltpu.VMEM((2, 4 * ROWS, HEAD), F32),
        pltpu.VMEM((2, 4 * ROWS, HEAD), F32),
        pltpu.VMEM((4 * ROWS, SLOTS), F32),
        pltpu.VMEM((4 * ROWS, SLOTS), BF16),
        pltpu.VMEM((4 * ROWS, HEAD), F32),
        pltpu.VMEM((2, 2 * ROWS, 256), BF16),
        pltpu.VMEM((XS, 2 * ROWS, PARTS[0][1]), F32),
        pltpu.VMEM((2, ROWS, 128), BF16),
        pltpu.VMEM((TP, ROWS, 128), BF16),
        pltpu.VMEM((CHIPS, ROWS, BLOCK), BF16),
        pltpu.VMEM((CHIPS, ROWS, BLOCK), BF16),
        dma((32,)),
        dma((DP,)), dma((DP,)), dma((8,)), dma((8,)), dma((8,)), dma((8,)),
        dma((TP,)), dma((12,)), dma((3,)), dma((3,)),
        dma((TP,)), dma((TP,)), *[dma((len(PARTS), CHIPS))] * 6,
    ]
    hidden = ((2, ROWS, WIDTH), BF16)
    squares = ((2, ROWS, 128), F32)
    row = ((1, WIDTH), F32)
    pair = ((2, 2, ROWS, HEAD), BF16)
    args = (
        tokens_in, attn_gain.reshape(1, WIDTH), post_gain.reshape(1, WIDTH), w_query,
        key_weight_base, value_weight_base, w_out, left_qkv.swapaxes(1, 2), right_query,
        right_key_value, left_out.T, right_out, kv_cache, lengths.reshape(1, ROWS),
        starts.reshape(1, ROWS),
    )
    results = pl.pallas_call(
        main_kernel,
        out_shape=tuple(pltpu.VMEM(*s) for s in (hidden, squares, row, pair)),
        in_specs=[hbm] * len(args),
        out_specs=(vmem,) * 4,
        scratch_shapes=scratch,
        compiler_params=pltpu.CompilerParams(
            collective_id=0, has_side_effects=True, vmem_limit_bytes=40 * 1024 * 1024),
    )(*[pltpu.with_memory_space_constraint(a, pltpu.HBM) for a in args])
    return pl.pallas_call(
        close_kernel,
        out_shape=tuple(jax.ShapeDtypeStruct(*s) for s in (hidden, hidden, pair)),
        in_specs=[vmem] * 4,
        out_specs=(hbm,) * 3,
        scratch_shapes=[pltpu.VMEM(*hidden), dma((6,))],
    )(*[pltpu.with_memory_space_constraint(a, pltpu.VMEM) for a in results])


def solution(mesh):
    in_specs = (
        P(None, "dp", None),
        P(),
        P(),
        P(None, "tensor"),
        P(None, "tensor"),
        P(None, "tensor"),
        P("tensor", None),
        P(None, "dp", None),
        P("dp", "tensor"),
        P(None, "dp", "tensor"),
        P("tensor", "dp"),
        P("dp", None),
        P(None, "dp", "tensor", None, None),
        P("dp"),
        P("dp"),
    )
    out_specs = (P(None, "dp", None), P(None, "dp", None), P(None, None, "dp", "tensor"))
    return jax.shard_map(shards, mesh=mesh, in_specs=in_specs, out_specs=out_specs, check_vma=False)
```

```python
import math

import jax
import jax.numpy as jnp
from jax import lax
from jax.experimental import pallas as pl
from jax.experimental.pallas import tpu as pltpu
from jax.sharding import PartitionSpec as P

MESH = pl.DeviceIdType.MESH
BF16 = jnp.bfloat16
F32 = jnp.float32

WIDTH = 5120
HEAD = 128
SLOTS = 320
WINDOW = 256
RANK = 64
ROWS = 24
DP = 16
TP = 16
CHIPS = 8
XS = 4
HALF = WIDTH // 2
BLOCK = HALF // XS
PARTS = ((0, 384), (384, 256))
LROWS = WIDTH // DP
LPAD = 384
NT = (((1,), (1,)), ((), ()))
TN = (((0,), (0,)), ((), ()))
NN = (((1,), (0,)), ((), ()))


def dot(a, b, dims=NN):
    return lax.dot_general(a, b, dims, preferred_element_type=F32)


def iota(shape, axis):
    return lax.broadcasted_iota(jnp.int32, shape, axis)


def one_hot(cond):
    return jnp.where(cond, 1.0, 0.0).astype(BF16)


def main_kernel(
    tok_in, gain_in, pgain_in, wq_in, wk_in, wv_in, wo_in, lqkv_in, rq_in, rkv_in, lo_in, ro_in,
    kv_in, len_in, start_in,
    hid_out, sq_out, pgain, kv_out,
    tok, gain, w, wo, kvc, lens, starts,
    lbuf, rq, rkv, lob, rob,
    lsend, lgat, pagat, pbgat, zgat, rbig, rmat,
    normed, proj, qs, kx, vx, score, att, attboth, keep, ysend, yall, csend, crecv,
    loc, lsend_sem, lrecv_sem, asend_sem, arecv_sem, psend_sem, precv_sem, zsend_sem, zrecv_sem,
    sib_send, sib_recv, ysend_sem, yrecv_sem, csend_sem, crecv_sem,
    gsend_sem, grecv_sem, fsend_sem, frecv_sem,
):
    dp = lax.axis_index("dp")
    tp = lax.axis_index("tensor")
    chip = tp // 2
    core = tp % 2
    zlo = chip // XS
    xpos = chip % XS
    yrow = dp // 4
    zhi = dp % 4
    lane8 = tp % 8
    sib = tp + 1 - 2 * core
    other = 1 - core
    ys = [(yrow + d) % 4 * 4 for d in range(4)]
    zs = [(zhi + d) % 4 for d in range(4)]
    xs = [(xpos + d) % XS for d in range(XS)]
    zlos = [zlo, 1 - zlo]
    cores = [core, other]
    zstep = jnp.where(zlo == 0, zs[3], zs[1])
    pend = {}

    def finish():
        for wait in pend.values():
            wait()

    def load(name, src, dst):
        c = pltpu.make_async_copy(src, dst, loc.at[len(pend)])
        c.start()
        pend[name] = c.wait

    def ready(*names):
        for name in names:
            pend.pop(name)()

    active = jnp.logical_or(zlo == 0, core == 0)
    slab = jnp.where(zlo == 0, lane8, 8 + lane8 // 2)
    mine = core * HALF + xpos * BLOCK
    rows = pl.ds(pl.multiple_of(16 * (lane8 % 4), 16), 16)
    load("l0", lqkv_in.at[lane8 // 4, rows], lbuf.at[0])
    load("l1", lqkv_in.at[2, pl.ds(pl.multiple_of(16 * (lane8 // 2), 16), 16)], lbuf.at[1])

    barrier = pltpu.get_barrier_semaphore()

    def greet(device):
        pl.semaphore_signal(barrier, inc=1, device_id=device, device_id_type=MESH)

    for dz, copy_at in ((2, zlos[1]), (1, 0), (3, 1), (0, zlo)):
        for dy in (2, 1, 3, 0):
            if dz or dy:
                greet({"dp": ys[dy] + zs[dz], "tensor": copy_at * 8 + lane8})
    for dz in (2, 1, 3):
        greet({"dp": ys[0] + zs[dz]})
    group = [(z, x, c) for x in (2, 1, 3, 0) for z in (1, 0) for c in (0, 1)][:-2]
    group = [p for p in group if any(p)] + [(0, 0, 1)]

    def member(p):
        return zlos[p[0]] * 8 + xs[p[1]] * 2 + cores[p[2]]

    for p in group:
        greet({"tensor": member(p)})

    load("rq", rq_in, rq)
    load("rkv", rkv_in, rkv)
    load("lo", lo_in, lob)
    load("ro", ro_in.at[:, pl.ds(pl.multiple_of(mine, 128), BLOCK)], rob)
    load("tok", tok_in, tok)
    load("gain", gain_in, gain)
    load("len", len_in, lens)
    load("start", start_in, starts)
    step = WIDTH // 4
    for i in range(4):
        rs = pl.ds(i * step, step)
        load(("wq", i), wq_in.at[rs], w.at[rs, 0:256])
        load(("wk", i), wk_in.at[rs], w.at[rs, 256:384])
        load(("wv", i), wv_in.at[rs], w.at[rs, 384:512])
    load("k", kv_in.at[0, :, 0], kvc.at[0])
    load("v", kv_in.at[1, :, 0], kvc.at[1])
    load("wo", wo_in.at[:, pl.ds(pl.multiple_of(core * HALF, 128), HALF)], wo.at[0:256])
    load("pgain", pgain_in, pgain)

    ready("l0", "l1")
    for k in range(2):
        rank_rows = jnp.concatenate([lbuf[k], jnp.zeros((16, LPAD - LROWS), F32)], 1)
        rank_rows = jnp.where(dp % 2 == 1, pltpu.roll(rank_rows, LPAD - LROWS, 1), rank_rows)
        lsend[k] = rank_rows.astype(BF16)
    lgat[dp] = lsend[zlo]

    pl.semaphore_wait(barrier, 15 + 15 + 3)

    def each_l(f):
        def to(k, dy, dp_z, to_zlo):
            if k or dy:
                f(pltpu.make_async_remote_copy(
                    lsend.at[to_zlo], lgat.at[dp], lsend_sem.at[4 * k + dy], lrecv_sem.at[dp],
                    device_id={"dp": ys[dy] + dp_z, "tensor": to_zlo * 8 + lane8},
                    device_id_type=MESH))

        @pl.when(jnp.logical_or(zlo == 1, core == 0))
        def _():
            for k, z in ((3, zs[2]), (2, zstep)):
                for dy in (2, 1, 3, 0):
                    to(k, dy, z, zlos[1])

        @pl.when(active)
        def _():
            for k, z in ((1, zstep), (0, zhi)):
                for dy in (2, 1, 3, 0):
                    to(k, dy, z, zlo)

    each_l(lambda c: c.start())
    pend["L", "sent"] = lambda: each_l(lambda c: c.wait_send())

    def ring(name, buf, send, recv, along_y):
        copies, waits = [], []
        for d in range(1, 4):
            if along_y:
                to = ys[d] + zhi
                src, came = buf.at[pl.ds(ys[0], 4)], buf.at[pl.ds(ys[4 - d], 4)]
            else:
                to = ys[0] + zs[d]
                src, came = buf.at[dp], buf.at[ys[0] + zs[4 - d]]
            k = d + 4 * along_y
            c = pltpu.make_async_remote_copy(
                src, src, send.at[k], recv.at[k], device_id={"dp": to}, device_id_type=MESH)
            copies.append(c)
            waits.append(pltpu.make_async_copy(came, came, recv.at[k]))
        for d in (2, 1, 3):
            copies[d - 1].start()
        pend[name, "sent"] = lambda: [c.wait_send() for c in copies]
        pend[name] = lambda: [c.wait() for c in waits]

    def when_active(f):
        @pl.when(active)
        def _():
            f()

    ready("rq", "rkv")
    tiles = [rq[:, 0:128], rq[:, 128:256], rkv[0], rkv[1]]
    pagat[dp] = jnp.concatenate(tiles, 0).astype(BF16)
    ring("Az", pagat, asend_sem, arecv_sem, False)
    ready("lo", "ro")
    tiles = [lob[:, 0:128], lob[:, 128:256]]
    tiles += [rob[:, 128 * i : 128 * (i + 1)] for i in range(5)]
    tiles += [jnp.zeros((4, 128), F32)]
    pbgat[dp] = jnp.concatenate(tiles, 0).astype(BF16)
    ring("Bz", pbgat, psend_sem, precv_sem, False)

    def to_sib(src, dst, k, name):
        c = pltpu.make_async_remote_copy(
            src, dst, sib_send.at[k], sib_recv.at[k],
            device_id={"tensor": sib}, device_id_type=MESH)
        c.start()
        pend[name, "sent"] = c.wait_send
        pend[name] = c.wait_recv

    to_sib(wo_in.at[:, pl.ds(pl.multiple_of(other * HALF, 128), HALF)], wo.at[256:512], 0, "wosib")


    ready("tok", "gain")
    sq = jnp.zeros((2, ROWS, 1), F32)
    for i in range(8):
        v = tok[:, :, i * 640 : (i + 1) * 640].astype(F32)
        sq = sq + jnp.sum(v * v, -1, keepdims=True)
    rs = lax.rsqrt(sq * (1.0 / WIDTH) + 1e-06)
    for i in range(8):
        cols = slice(i * 640, (i + 1) * 640)
        v = tok[:, :, cols].astype(F32) * rs * gain[:, cols][None]
        normed[:, cols] = v.reshape(2 * ROWS, 640).astype(BF16)

    acc = None
    for i in range(2):
        ready(("wq", i), ("wk", i), ("wv", i))
        part = dot(normed[:, i * step : (i + 1) * step], w[i * step : (i + 1) * step, :])
        acc = part if acc is None else acc + part
    proj[...] = acc

    ready("Az")
    ring("A", pagat, asend_sem, arecv_sem, True)

    def zcopy(k):
        return pltpu.make_async_remote_copy(
            zgat.at[slab], zgat.at[slab], zsend_sem.at[k], zrecv_sem.at[slab],
            device_id={"tensor": member(group[k])}, device_id_type=MESH)

    @pl.when(active)
    def _():
        z = jnp.zeros((16, 2 * ROWS), F32)
        for half in range(2):
            parts, cols = [], []
            for j in range(2 * half, DP, 4):
                for who in (j, j + 1):
                    @pl.when(dp != who)
                    def _():
                        mark = lgat.at[who]
                        pltpu.make_async_copy(mark, mark, lrecv_sem.at[who]).wait()

                parts += [lgat[j, :, 0:256], lgat[j, :, 256:384] + lgat[j + 1, :, 0:128]]
                parts += [lgat[j + 1, :, 128:384]]
                cols += [normed[:, LROWS * j : LROWS * (j + 2)]]
            z = z + dot(jnp.concatenate(parts, 1), jnp.concatenate(cols, 1), NT)
        z = jnp.concatenate([z, jnp.zeros((16, 128 - 2 * ROWS), F32)], 1)
        zgat[slab] = z.astype(BF16)

        for k in range(TP - 1):
            zcopy(k).start()

    def sent_z():
        @pl.when(active)
        def _():
            for k in range(TP - 1):
                zcopy(k).wait_send()

    def got_z():
        def got(s, _):
            src = jnp.where(s < 8, s, 2 * s - 8)

            @pl.when(src != tp)
            def _():
                pltpu.make_async_copy(zgat.at[s], zgat.at[s], zrecv_sem.at[s]).wait()

            return 0

        lax.fori_loop(0, 12, got, 0)

    pend["Z", "sent"] = sent_z
    pend["Z"] = got_z
    ready("Bz")
    ring("B", pbgat, psend_sem, precv_sem, True)
    acc = proj[...]
    for i in range(2, 4):
        ready(("wq", i), ("wk", i), ("wv", i))
        acc = acc + dot(normed[:, i * step : (i + 1) * step], w[i * step : (i + 1) * step, :])
    proj[...] = acc

    ready("len", "start")
    lenf = lens[...].astype(F32)
    stf = starts[...].astype(F32)

    def column(values, rows, owner):
        hit = owner(iota((rows, ROWS), 0)) == iota((rows, ROWS), 1)
        return jnp.sum(jnp.where(hit, values, 0.0), -1, keepdims=True)

    row = iota((2 * ROWS, 1), 0)
    pos = column(lenf, 2 * ROWS, lambda r: r % ROWS) + jnp.where(row >= ROWS, 1.0, 0.0)
    lane = iota((1, HEAD), 1)
    freq = jnp.exp((lane % 64).astype(F32) * (-2.0 * math.log(1000000.0) / HEAD))
    angle = pos * freq
    cos = jnp.cos(angle)
    sin = jnp.sin(angle) * jnp.where(lane < 64, -1.0, 1.0)

    def rope(v):
        return v * cos + pltpu.roll(v, 64, 1) * sin

    arow = iota((4 * ROWS, 1), 0)
    tokstep = jnp.where(arow % 4 >= 2, 1.0, 0.0)
    alen = column(lenf, 4 * ROWS, lambda r: r // 4)
    ast = column(stf, 4 * ROWS, lambda r: r // 4)
    slot = iota((4 * ROWS, SLOTS), 1).astype(F32) - ast
    slot = jnp.where(slot < 0, slot + float(SLOTS), slot)
    visible = jnp.logical_and(slot < alen, alen + tokstep - slot < float(WINDOW))

    ready("A")
    o = iota((256, 256), 0)
    perm = one_hot(iota((256, 256), 1) == ((o % 64) // 4) * 16 + 4 * (o // 64) + o % 4)
    right = dot(perm, pagat[...].reshape(256, 128)).astype(BF16)
    rbig[...] = jnp.zeros_like(rbig)
    for t, p in enumerate((0, 0, 1, 2)):
        rbig[64 * p : 64 * (p + 1), 128 * t : 128 * (t + 1)] = right[64 * t : 64 * (t + 1)]

    ready(("L", "sent"), ("Az", "sent"), ("wosib", "sent"))
    ready("Z")
    delta = dot(zgat[...].reshape(3 * RANK, 128), rbig[...], TN)[: 2 * ROWS]
    delta = proj[...] + 0.5 * delta
    cols = [delta[:, 128 * t : 128 * (t + 1)] for t in range(4)]
    rounded = [rope(cols[0]), rope(cols[1]), rope(cols[2]), cols[3]]
    rounded = [v.astype(BF16).astype(F32) for v in rounded]
    for t in range(2):
        rows = slice(t * ROWS, (t + 1) * ROWS)
        kv_out[t, 0] = rounded[2][rows].astype(BF16)
        kv_out[t, 1] = rounded[3][rows].astype(BF16)
        for g in range(2):
            qs[pl.ds(2 * t + g, ROWS, stride=4), :] = rounded[g][rows]
        for r in range(4):
            kx[t, pl.ds(r, ROWS, stride=4), :] = rounded[2][rows]
            vx[t, pl.ds(r, ROWS, stride=4), :] = rounded[3][rows]

    scale = 1.0 / math.sqrt(HEAD)
    ready("k")
    odd = iota((8, 1), 0) >= 4
    for i in range(ROWS // 2):
        q = qs[8 * i : 8 * (i + 1), :]
        q = jnp.concatenate([jnp.where(odd, 0.0, q), jnp.where(odd, q, 0.0)], 1).astype(BF16)
        k = jnp.concatenate([kvc[0, 2 * i], kvc[0, 2 * i + 1]], 1)
        score[8 * i : 8 * (i + 1), :] = dot(q, k, NT)
    sc = jnp.where(visible, score[...] * scale, -1e30)
    q = qs[...]
    f0 = jnp.sum(q * kx[0], -1, keepdims=True) * scale
    f1 = jnp.sum(q * kx[1], -1, keepdims=True) * scale
    f1 = jnp.where(tokstep > 0.5, f1, -1e30)
    top = jnp.maximum(jnp.max(sc, -1, keepdims=True), jnp.maximum(f0, f1))
    ex = jnp.exp(sc - top)
    e0 = jnp.exp(f0 - top)
    e1 = jnp.exp(f1 - top)
    den = jnp.sum(ex, -1, keepdims=True) + (e0 + e1)
    score[...] = ex / den
    p0 = (e0 / den).astype(BF16).astype(F32)
    p1 = (e1 / den).astype(BF16).astype(F32)
    att[...] = p0 * vx[0] + p1 * vx[1]
    ready("v")
    for i in range(ROWS // 2):
        rows = slice(8 * i, 8 * (i + 1))
        v = jnp.concatenate([kvc[1, 2 * i], kvc[1, 2 * i + 1]], 1)
        s = dot(score[rows, :].astype(BF16), v)
        att[rows, :] = att[rows, :] + jnp.where(odd, s[:, 128:256], s[:, 0:128])
    heads = []
    for g in range(2):
        heads.append(jnp.concatenate([att[pl.ds(2 * t + g, ROWS, stride=4), :] for t in range(2)], 0))
    attboth[0] = jnp.concatenate(heads, 1).astype(BF16)

    to_sib(attboth.at[0], attboth.at[1], 1, "att")
    own = attboth[0]
    ready("B")
    rmat[0] = dot(perm, pbgat[:, 0:16, :].reshape(256, 128)).astype(BF16)
    lot = jnp.concatenate([rmat[0, 0:64], rmat[0, 64:128]], 1)
    y = dot(own, lot, NT)
    y = jnp.concatenate([y, jnp.zeros((2 * ROWS, 128 - RANK), F32)], 1)
    ysend[0] = y[0:ROWS].astype(BF16)
    ysend[1] = y[ROWS:].astype(BF16)

    def ycopy(k):
        return pltpu.make_async_remote_copy(
            ysend.at[zlos[group[k][0]]], yall.at[tp], ysend_sem.at[k], yrecv_sem.at[tp],
            device_id={"tensor": member(group[k])}, device_id_type=MESH)

    for k in range(TP - 1):
        ycopy(k).start()
    pend["Y", "sent"] = lambda: [ycopy(k).wait_send() for k in range(TP - 1)]

    ready("wo")
    for n in (2, 1, 3, 0):
        cols = pl.ds(pl.multiple_of(xs[n] * BLOCK, 128), PARTS[0][1])
        keep[n] = dot(own, wo[0:256, cols])

    offsets = ((1, 2), (0, 2), (1, 1), (1, 3), (0, 1), (0, 3), (1, 0))

    def at(o):
        return zlos[o[0]] * XS + xs[o[1]]

    def source(o):
        return zlos[o[0]] * XS + xs[-o[1]]

    def ccopy(c, h):
        cols = pl.ds(*PARTS[h])
        return pltpu.make_async_remote_copy(
            csend.at[c, :, cols], crecv.at[chip, :, cols], csend_sem.at[h, c], crecv_sem.at[h, chip],
            device_id={"tensor": 2 * c + core}, device_id_type=MESH)

    ready("wosib", "att")
    theirs = attboth[1]
    both = jnp.concatenate([own, theirs], 1)
    total = []
    for h, (first, width) in enumerate(PARTS):
        for n in (2, 1, 3, 0):
            x = xs[n]
            cols = pl.ds(pl.multiple_of(x * BLOCK + first, 128), width)
            part = keep[n] + dot(theirs, wo[256:512, cols]) if h == 0 else dot(both, wo[:, cols])
            for t in range(2):
                csend[t * XS + x, :, first : first + width] = part[t * ROWS : (t + 1) * ROWS].astype(BF16)
            ccopy(zlos[1] * XS + x, h).start()
            if n != 0:
                ccopy(zlo * XS + x, h).start()
            else:
                total.append(jnp.where(zlo == 0, part[0:ROWS], part[ROWS:]))
    rmat[1] = dot(perm, pbgat[:, 16:32, :].reshape(256, 128)).astype(BF16)
    pend["C", "sent"] = lambda: [ccopy(at(o), h).wait_send() for o in offsets for h in range(len(PARTS))]

    ready(("A", "sent"), ("Bz", "sent"), ("B", "sent"), ("Z", "sent"), ("att", "sent"))
    ysum = jnp.where(zlo == 0, y[0:ROWS], y[ROWS:])
    for p in group[::-1]:
        src = member(p)
        pltpu.make_async_copy(yall.at[src], yall.at[src], yrecv_sem.at[src]).wait()
        ysum = ysum + yall[src].astype(F32)
    ysum = (0.5 * ysum[:, 0:RANK]).astype(BF16)
    ro = jnp.concatenate(
        [rmat[0, 128:192, :], rmat[0, 192:256, :], rmat[1, 0:64, :], rmat[1, 64:128, :],
         rmat[1, 128:192, :]], 1)

    def block(k, c, h):
        return hid_out.at[c // XS, :, pl.ds(
            pl.multiple_of(k * HALF + c % XS * BLOCK + PARTS[h][0], 128), PARTS[h][1])]

    def gcopy(c, h):
        return pltpu.make_async_remote_copy(
            block(core, chip, h), block(core, chip, h), gsend_sem.at[h, c], grecv_sem.at[h, chip],
            device_id={"tensor": 2 * c + core}, device_id_type=MESH)

    def fcopy(c, h):
        return pltpu.make_async_remote_copy(
            block(core, c, h), block(core, c, h), fsend_sem.at[h, c], frecv_sem.at[h, c],
            device_id={"tensor": sib}, device_id_type=MESH)

    def squares(v):
        v = v.astype(F32)
        v = v * v
        return sum(v[:, i : i + 128] for i in range(0, v.shape[1], 128))

    sq = [jnp.zeros((ROWS, 128), F32) for _ in range(2)]
    for h, (first, width) in enumerate(PARTS):
        here = pl.ds(pl.multiple_of(mine + first, 128), width)
        out = total[h] + tok[zlo, :, here].astype(F32) + dot(ysum, ro[:, first : first + width])
        cols = pl.ds(first, width)
        for o in offsets[::-1]:
            src = source(o)
            mark = crecv.at[src, :, cols]
            pltpu.make_async_copy(mark, mark, crecv_sem.at[h, src]).wait()
            out = out + mark[...].astype(F32)
        out = out.astype(BF16)
        hid_out[zlo, :, here] = out
        sq[0] = sq[0] + squares(out)
        for o in offsets:
            gcopy(at(o), h).start()
        fcopy(chip, h).start()
    pend["G", "sent"] = lambda: [gcopy(at(o), h).wait_send() for o in offsets for h in range(len(PARTS))]
    every = ((0, 0),) + offsets[::-1]
    ready(("Y", "sent"), ("C", "sent"))
    pend["F", "sent"] = lambda: [fcopy(source(o), h).wait_send() for o in every for h in range(len(PARTS))]
    for h in range(len(PARTS)):
        for o in offsets[::-1]:
            mark = block(core, source(o), h)
            pltpu.make_async_copy(mark, mark, grecv_sem.at[h, source(o)]).wait()
            fcopy(source(o), h).start()
            sq[o[0]] = sq[o[0]] + squares(mark[...])
    ready(("G", "sent"))
    for h in range(len(PARTS)):
        for o in every:
            mark = block(other, source(o), h)
            pltpu.make_async_copy(mark, mark, frecv_sem.at[h, source(o)]).wait()
            sq[o[0]] = sq[o[0]] + squares(mark[...])

    ready("pgain")
    for t in range(2):
        sq_out[t] = jnp.where(zlo == t, sq[0], sq[1])

    finish()


def close_kernel(hid, sq, gain, kv, hid_out, mlp_out, kv_out, mlp, sems):
    copies = []

    def send(src, dst):
        c = pltpu.make_async_copy(src, dst, sems.at[len(copies)])
        c.start()
        copies.append(c)

    send(hid, hid_out)
    send(kv, kv_out)
    for t in range(2):
        rs = lax.rsqrt(jnp.sum(sq[t], -1, keepdims=True) * (1.0 / WIDTH) + 1e-06)
        for half in range(2):
            for i in range(4 * half, 4 * half + 4):
                cols = slice(i * 640, (i + 1) * 640)
                mlp[t, :, cols] = (hid[t, :, cols].astype(F32) * rs * gain[:, cols]).astype(BF16)
            part = pl.ds(half * HALF, HALF)
            send(mlp.at[t, :, part], mlp_out.at[t, :, part])
    for c in copies:
        c.wait()


def shards(
    tokens_in, attn_gain, post_gain, w_query, key_weight_base, value_weight_base, w_out, left_qkv,
    right_query, right_key_value, left_out, right_out, kv_cache, lengths, starts,
):
    hbm = pl.BlockSpec(memory_space=pltpu.HBM)
    vmem = pl.BlockSpec(memory_space=pltpu.VMEM)
    dma = pltpu.SemaphoreType.DMA
    scratch = [
        pltpu.VMEM((2, ROWS, WIDTH), BF16),
        pltpu.VMEM((1, WIDTH), F32),
        pltpu.VMEM((WIDTH, 512), BF16),
        pltpu.VMEM((512, HALF), BF16),
        pltpu.VMEM((2, ROWS, SLOTS, HEAD), BF16),
        pltpu.VMEM((1, ROWS), jnp.int32),
        pltpu.VMEM((1, ROWS), jnp.int32),
        pltpu.VMEM((2, 16, LROWS), F32),
        pltpu.VMEM((4, 256), F32),
        pltpu.VMEM((2, 4, 128), F32),
        pltpu.VMEM((4, 256), F32),
        pltpu.VMEM((4, BLOCK), F32),
        pltpu.VMEM((2, 16, LPAD), BF16),
        pltpu.VMEM((DP, 16, LPAD), BF16),
        pltpu.VMEM((DP, 16, 128), BF16),
        pltpu.VMEM((DP, 32, 128), BF16),
        pltpu.VMEM((12, 16, 128), BF16),
        pltpu.VMEM((3 * RANK, 512), BF16),
        pltpu.VMEM((2, 256, 128), BF16),
        pltpu.VMEM((2 * ROWS, WIDTH), BF16),
        pltpu.VMEM((2 * ROWS, 512), F32),
        pltpu.VMEM((4 * ROWS, HEAD), F32),
        pltpu.VMEM((2, 4 * ROWS, HEAD), F32),
        pltpu.VMEM((2, 4 * ROWS, HEAD), F32),
        pltpu.VMEM((4 * ROWS, SLOTS), F32),
        pltpu.VMEM((4 * ROWS, HEAD), F32),
        pltpu.VMEM((2, 2 * ROWS, 256), BF16),
        pltpu.VMEM((XS, 2 * ROWS, PARTS[0][1]), F32),
        pltpu.VMEM((2, ROWS, 128), BF16),
        pltpu.VMEM((TP, ROWS, 128), BF16),
        pltpu.VMEM((CHIPS, ROWS, BLOCK), BF16),
        pltpu.VMEM((CHIPS, ROWS, BLOCK), BF16),
        dma((32,)),
        dma((DP,)), dma((DP,)), dma((8,)), dma((8,)), dma((8,)), dma((8,)),
        dma((TP,)), dma((12,)), dma((3,)), dma((3,)),
        dma((TP,)), dma((TP,)), *[dma((len(PARTS), CHIPS))] * 6,
    ]
    hidden = ((2, ROWS, WIDTH), BF16)
    squares = ((2, ROWS, 128), F32)
    row = ((1, WIDTH), F32)
    pair = ((2, 2, ROWS, HEAD), BF16)
    args = (
        tokens_in, attn_gain.reshape(1, WIDTH), post_gain.reshape(1, WIDTH), w_query,
        key_weight_base, value_weight_base, w_out, left_qkv.swapaxes(1, 2), right_query,
        right_key_value, left_out.T, right_out, kv_cache, lengths.reshape(1, ROWS),
        starts.reshape(1, ROWS),
    )
    results = pl.pallas_call(
        main_kernel,
        out_shape=tuple(pltpu.VMEM(*s) for s in (hidden, squares, row, pair)),
        in_specs=[hbm] * len(args),
        out_specs=(vmem,) * 4,
        scratch_shapes=scratch,
        compiler_params=pltpu.CompilerParams(
            collective_id=0, has_side_effects=True, vmem_limit_bytes=40 * 1024 * 1024),
    )(*[pltpu.with_memory_space_constraint(a, pltpu.HBM) for a in args])
    return pl.pallas_call(
        close_kernel,
        out_shape=tuple(jax.ShapeDtypeStruct(*s) for s in (hidden, hidden, pair)),
        in_specs=[vmem] * 4,
        out_specs=(hbm,) * 3,
        scratch_shapes=[pltpu.VMEM(*hidden), dma((6,))],
    )(*[pltpu.with_memory_space_constraint(a, pltpu.VMEM) for a in results])


def solution(mesh):
    in_specs = (
        P(None, "dp", None),
        P(),
        P(),
        P(None, "tensor"),
        P(None, "tensor"),
        P(None, "tensor"),
        P("tensor", None),
        P(None, "dp", None),
        P("dp", "tensor"),
        P(None, "dp", "tensor"),
        P("tensor", "dp"),
        P("dp", None),
        P(None, "dp", "tensor", None, None),
        P("dp"),
        P("dp"),
    )
    out_specs = (P(None, "dp", None), P(None, "dp", None), P(None, None, "dp", "tensor"))
    return jax.shard_map(shards, mesh=mesh, in_specs=in_specs, out_specs=out_specs, check_vma=False)
```
